256 devices in a mesh: shape: 4 (over y), space: 64 (over x, z, core).
Axes of the slice: x: 4, y: 4, z: 8, core: 2. Of those that a mesh axis runs over, the one named last changes fastest.
Arguments:
- features: bfloat16 [4, 128, 512, 128], P('shape', 'space'), may hold values from -45 to 45
- gain_one: float32 [128], replicated, may hold values from 0.1 to 1.9
- weight_one: bfloat16 [7, 128, 128], replicated, may hold values from -0.1875 to 0.1875
- gain_two: float32 [128], replicated, may hold values from 0.1 to 1.9
- weight_two: bfloat16 [7, 128, 128], replicated, may hold values from -0.1875 to 0.1875
- live: int32 [4, 128], P('shape', 'space'), may hold values from 0 to 1, as said below
- send_index: int32 [4, 64, 64, 1], P('shape', 'space'), may hold values from -1 to 11, as said below
- recv_index: int32 [4, 128, 6], P('shape', 'space'), may hold values from -1 to 63, as said below
- cotangent: bfloat16 [4, 128, 512, 128], P('shape', 'space'), may hold values from -6 to 6
Outputs:
- output: bfloat16 [4, 128, 512, 128], P('shape', 'space')
- grad_features: bfloat16 [4, 128, 512, 128], P('shape', 'space')
- grad_weight_one: float32 [7, 128, 128], replicated
- grad_weight_two: float32 [7, 128, 128], replicated
- grad_gain_one: float32 [128], replicated
- grad_gain_two: float32 [128], replicated
The draws below stay inside these ranges and needn't reach their ends.
Inputs may be any that keep to these rules, and one draw needn't show every extreme that they name: The live slots of each device are its first ones, at least 1 of them; in every shape one device has both slots live and another only 1. `recv_index`: -1 where the face has no neighbour slab, always so on slots that are not live; else a position r of the device's receive buffer of 64 slabs, r being the sending device (one slab per sender). No two faces of one device share a position; on every device the slot from some sender is in use; slot 0 of every device has all six faces. send_index[s, d, e, c] is -1 where slot c from device d to device e is unused, else 6 b + f for a live slot b of device d, f being the opposite of the face of the brick of e that reads that slot; it agrees with recv_index.
All inputs are finite; a program needn't handle non-finite values.
Results may differ from the reference program's by a relative error of at most 0.014.
Values may be sent and summed in bfloat16 or wider, within the bound.
A program may use at most 64 MiB of HBM per device.

```python
import math
import jax
import jax.numpy as jnp
from jax import lax

C = 128
EDGE = 8
TAPS = 7
B_DEV = 2
VOX = 512
SHAPES = 4
PEERS = 64
BRICKS = 128
CAP = 1


def brick_layout(key):
    positions = PEERS * CAP
    low_live = max(1, B_DEV // 2)
    subkeys = jax.random.split(jax.random.fold_in(key, 7301), 6)
    live_count = jax.random.randint(subkeys[0], (SHAPES, PEERS), low_live, B_DEV + 1).astype(jnp.int32)
    full_device = jnp.full((SHAPES,), PEERS - 1, jnp.int32)
    sparse_device = jax.random.randint(subkeys[1], (SHAPES,), 0, PEERS - 1).astype(jnp.int32)
    device_ids = jnp.arange(PEERS, dtype=jnp.int32)[None, :]
    live_count = jnp.where(device_ids == full_device[:, None], B_DEV, live_count)
    live_count = jnp.where(device_ids == sparse_device[:, None], low_live, live_count)
    slot_ids = jnp.arange(B_DEV, dtype=jnp.int32)
    live_slots = (slot_ids[None, None, :] < live_count[:, :, None]).astype(jnp.int32)
    face_draw = jax.random.randint(subkeys[2], (SHAPES, PEERS, B_DEV, 6), 0, 4)
    has_face = (face_draw > 0) | (slot_ids[None, None, :, None] < low_live)
    has_face = has_face & (live_slots[..., None] > 0)
    flat_face = has_face.reshape(SHAPES, PEERS, B_DEV * 6).astype(jnp.int32)
    entry_ids = jnp.arange(B_DEV * 6, dtype=jnp.int32)
    forced_entry = (entry_ids == 4)[None, None, :]
    ranked_face = jnp.where(forced_entry, 0, flat_face)
    rank_index = jnp.cumsum(ranked_face, axis=-1) - 1
    full_peer = jax.random.randint(subkeys[3], (SHAPES, PEERS), 0, PEERS).astype(jnp.int32)
    position_ids = jnp.arange(positions, dtype=jnp.int32)
    noise_draw = jax.random.randint(subkeys[4], (SHAPES, PEERS, positions), 0, 1 << 20).astype(jnp.int32)
    outside = (position_ids[None, None, :] // CAP != full_peer[:, :, None]).astype(jnp.int32)
    is_last = (position_ids == positions - 1).astype(jnp.int32)[None, None, :]
    tier = jnp.maximum(outside, 0) + 2 * is_last
    score = (tier * (1 << 20) + noise_draw) * positions + position_ids[None, None, :]
    order_index = jnp.argsort(score, axis=-1).astype(jnp.int32)
    place = jnp.take_along_axis(order_index, jnp.maximum(rank_index, 0), axis=-1)
    place = jnp.where(flat_face > 0, place, -1).astype(jnp.int32)
    place = jnp.where(forced_entry, positions - 1, place).astype(jnp.int32)
    sender = jnp.maximum(place, 0) // CAP
    sender_live = jnp.take_along_axis(live_count, sender.reshape(SHAPES, -1), axis=1).reshape(sender.shape)
    pick_draw = jax.random.randint(subkeys[5], place.shape, 0, 1 << 16).astype(jnp.int32)
    source_slot = jnp.where(forced_entry, sender_live - 1, pick_draw % sender_live)
    face_ids = entry_ids % 6
    opposite = face_ids + 1 - 2 * (face_ids % 2)
    send_code = source_slot * 6 + opposite[None, None, :]
    table = jnp.full((SHAPES, PEERS, positions + 1), -1, jnp.int32)
    target = jnp.where(place >= 0, place, positions)
    shape_idx = jnp.arange(SHAPES, dtype=jnp.int32)[:, None, None]
    recv_idx = jnp.arange(PEERS, dtype=jnp.int32)[None, :, None]
    table = table.at[shape_idx, recv_idx, target].set(jnp.where(place >= 0, send_code, -1).astype(jnp.int32))
    send_table = table[:, :, :positions].reshape(SHAPES, PEERS, PEERS, CAP).transpose(0, 2, 1, 3)
    recv_table = place.reshape(SHAPES, PEERS * B_DEV, 6)
    return (live_slots.reshape(SHAPES, PEERS * B_DEV), send_table, recv_table)


def draw_live(key, part):
    return brick_layout(key)[0]


def draw_send_index(key, part):
    return brick_layout(key)[1]


def draw_recv_index(key, part):
    return brick_layout(key)[2]


def draw_features(key, part):
    subkeys = jax.random.split(jax.random.fold_in(key, 911), 3)
    row_scale = jnp.exp(jax.random.uniform(subkeys[0], (SHAPES, BRICKS, VOX, 1), minval=math.log(0.3), maxval=math.log(3.0)))
    chan_scale = jnp.exp(jax.random.uniform(subkeys[1], (C,), minval=math.log(0.3), maxval=math.log(3.0)))
    base_draw = jnp.clip(jax.random.normal(subkeys[2], (SHAPES, BRICKS, VOX, C)), -5.0, 5.0)
    values = base_draw * row_scale * chan_scale
    return values.astype(jnp.bfloat16)


def levels(stream_key, extent, cuts, smallest, top_value):
    def one(dim, shards_of):
        steps = jax.random.uniform(jax.random.fold_in(jax.random.fold_in(stream_key, 6), dim), (shards_of,), jnp.float32, smallest / len(cuts), top_value / len(cuts))
        return jnp.repeat(jnp.exp(steps), extent[dim] // shards_of).reshape((-1,) + (1,) * (len(extent) - dim - 1))

    level = one(*cuts[0])
    for cut in cuts[1:]:
        level = level * one(*cut)
    return level


def scatter_about(key, shape, scale, most, shards=(), held_as=jnp.bfloat16):
    result = scale * jax.random.normal(key, shape, jnp.float32)
    if shards:
        result = result * levels(key, shape, shards, -0.22, 0.18)
    return jnp.clip(result, -most, most).astype(held_as)


def setup_inputs(seed: int = 0) -> dict:
    keys = jax.random.split(jax.random.key(seed), 10)
    return {
        "features": draw_features(jax.random.fold_in(keys[9], 71), 0),
        "gain_one": jnp.clip(1.0 + 0.18 * jax.random.normal(keys[1], (C,), jnp.float32), 0.1, 1.9),
        "weight_one": scatter_about(keys[2], (TAPS, C, C), (TAPS * C) ** -0.5, 0.1875),
        "gain_two": jnp.clip(1.0 + 0.18 * jax.random.normal(keys[3], (C,), jnp.float32), 0.1, 1.9),
        "weight_two": scatter_about(keys[4], (TAPS, C, C), (TAPS * C) ** -0.5, 0.1875),
        "live": draw_live(jax.random.fold_in(keys[9], 71), 0),
        "send_index": draw_send_index(jax.random.fold_in(keys[9], 71), 0),
        "recv_index": draw_recv_index(jax.random.fold_in(keys[9], 71), 0),
        "cotangent": scatter_about(keys[8], (SHAPES, BRICKS, VOX, C), 1.0, 6.0, ((0, 4), (1, 64))),
    }


OFFSETS = ((0, 0, 0), (-1, 0, 0), (1, 0, 0), (0, -1, 0), (0, 1, 0), (0, 0, -1), (0, 0, 1))
norm_epsilon = 1e-05

def pre_act(values, gain):
    row_mean = lax.optimization_barrier(jnp.mean(values, axis=-1, keepdims=True))
    centered = values - row_mean
    variance = lax.optimization_barrier(jnp.mean(centered * centered, axis=-1, keepdims=True))
    return jax.nn.silu(centered * lax.rsqrt(variance + norm_epsilon) * gain)

def pre_back(brick_cube, gain, upstream):
    outputs, pullback = jax.vjp(pre_act, brick_cube.astype(jnp.float32), gain)
    return pullback(upstream)

def face_slabs(brick_cube):
    brick_count = brick_cube.shape[0]
    edge_len = brick_cube.shape[1]
    last_layer = edge_len - 1
    face_list = [brick_cube[:, 0], brick_cube[:, last_layer], brick_cube[:, :, 0], brick_cube[:, :, last_layer], brick_cube[:, :, :, 0], brick_cube[:, :, :, last_layer]]
    return jnp.stack([face_part.reshape(brick_count, edge_len * edge_len, brick_cube.shape[-1]) for face_part in face_list], axis=1)

def pad_cube(brick_cube, halo_slabs):
    brick_count = brick_cube.shape[0]
    edge_len = brick_cube.shape[1]
    channels = brick_cube.shape[-1]
    slab_grid = halo_slabs.reshape(brick_count, 6, edge_len, edge_len, channels)
    far_side = edge_len + 1
    inside = slice(1, far_side)
    padded = jnp.pad(brick_cube, ((0, 0), (1, 1), (1, 1), (1, 1), (0, 0)))
    padded = padded.at[:, 0, inside, inside].set(slab_grid[:, 0])
    padded = padded.at[:, far_side, inside, inside].set(slab_grid[:, 1])
    padded = padded.at[:, inside, 0, inside].set(slab_grid[:, 2])
    padded = padded.at[:, inside, far_side, inside].set(slab_grid[:, 3])
    padded = padded.at[:, inside, inside, 0].set(slab_grid[:, 4])
    padded = padded.at[:, inside, inside, far_side].set(slab_grid[:, 5])
    return padded

def add_faces(volume, face_terms):
    brick_count = volume.shape[0]
    edge_len = volume.shape[1]
    channels = volume.shape[-1]
    term_grid = face_terms.reshape(brick_count, 6, edge_len, edge_len, channels)
    last_layer = edge_len - 1
    volume = volume.at[:, 0].add(term_grid[:, 0])
    volume = volume.at[:, last_layer].add(term_grid[:, 1])
    volume = volume.at[:, :, 0].add(term_grid[:, 2])
    volume = volume.at[:, :, last_layer].add(term_grid[:, 3])
    volume = volume.at[:, :, :, 0].add(term_grid[:, 4])
    volume = volume.at[:, :, :, last_layer].add(term_grid[:, 5])
    return volume

def shifted(padded, tap_index):
    step_i, step_j, step_k = OFFSETS[tap_index]
    edge_len = padded.shape[1] - 2
    window = padded[:, 1 + step_i:1 + step_i + edge_len, 1 + step_j:1 + step_j + edge_len, 1 + step_k:1 + step_k + edge_len]
    return window.reshape(-1, padded.shape[-1])

def convolve(padded, weight):
    running = jnp.dot(shifted(padded, 0), weight[0], preferred_element_type=jnp.float32)
    for tap_index in range(1, len(OFFSETS)):
        running = running + jnp.dot(shifted(padded, tap_index), weight[tap_index], preferred_element_type=jnp.float32)
    return running

def conv_back(padded, grad_rows, weight):
    brick_count = padded.shape[0]
    edge_len = padded.shape[1] - 2
    channels = padded.shape[-1]
    weight_grad = jnp.stack([lax.dot_general(shifted(padded, tap_index), grad_rows, (((0,), (0,)), ((), ())), preferred_element_type=jnp.float32) for tap_index in range(len(OFFSETS))])
    spread = jnp.zeros(padded.shape, jnp.float32)
    for tap_index in range(len(OFFSETS)):
        step_i, step_j, step_k = OFFSETS[tap_index]
        tap_term = lax.dot_general(grad_rows, weight[tap_index], (((1,), (1,)), ((), ())), preferred_element_type=jnp.float32)
        tap_term = tap_term.reshape(brick_count, edge_len, edge_len, edge_len, channels)
        spread = spread.at[:, 1 + step_i:1 + step_i + edge_len, 1 + step_j:1 + step_j + edge_len, 1 + step_k:1 + step_k + edge_len].add(tap_term)
    far_side = edge_len + 1
    inside = slice(1, far_side)
    interior = spread[:, inside, inside, inside]
    face_list = [spread[:, 0, inside, inside], spread[:, far_side, inside, inside], spread[:, inside, 0, inside], spread[:, inside, far_side, inside], spread[:, inside, inside, 0], spread[:, inside, inside, far_side]]
    halo_grad = jnp.stack([face_part.reshape(brick_count, edge_len * edge_len, channels) for face_part in face_list], axis=1).astype(jnp.bfloat16)
    return (weight_grad, interior, halo_grad)

def find_sources(send_index, recv_index):
    shape_ids = jnp.arange(SHAPES, dtype=jnp.int32)[:, None, None]
    receiver = (jnp.arange(BRICKS, dtype=jnp.int32) // B_DEV)[None, :, None]
    has_source = recv_index >= 0
    position = jnp.maximum(recv_index, 0).astype(jnp.int32)
    sender = position // CAP
    slot_index = position % CAP
    send_code = jnp.maximum(send_index[shape_ids, sender, receiver, slot_index], 0).astype(jnp.int32)
    source_brick = shape_ids * BRICKS + sender * B_DEV + send_code // 6
    source_face = send_code % 6
    total_bricks = SHAPES * BRICKS
    return (source_brick.reshape(total_bricks, 6), source_face.reshape(total_bricks, 6), has_source.reshape(total_bricks, 6))

def gather_halos(brick_cube, source_brick, source_face, has_source):
    face_rows = face_slabs(brick_cube)
    picked = face_rows[source_brick, source_face]
    return jnp.where(has_source[:, :, None, None], picked, jnp.zeros_like(picked))

def return_grads(halo_grad, source_brick, source_face, has_source):
    sent_back = jnp.where(has_source[:, :, None, None], halo_grad.astype(jnp.float32), jnp.zeros(halo_grad.shape, jnp.float32))
    running = jnp.zeros(halo_grad.shape, jnp.float32)
    return running.at[source_brick, source_face].add(sent_back)

def reference(features, gain_one, weight_one, gain_two, weight_two, live, send_index, recv_index, cotangent):
    edge_len = EDGE
    channels = C
    total_bricks = SHAPES * BRICKS
    groups = total_bricks // B_DEV
    cube_shape = (groups, B_DEV, edge_len, edge_len, edge_len, channels)
    flat_shape = (total_bricks, edge_len, edge_len, edge_len, channels)
    halo_shape = (groups, B_DEV, 6, edge_len * edge_len, channels)
    source_brick, source_face, has_source = find_sources(send_index, recv_index)
    cubes_in = features.reshape(cube_shape)
    alive_mask = live.reshape(groups, B_DEV) > 0
    cot_cubes = cotangent.reshape(cube_shape)

    def activate_one(brick_cube):
        return pre_act(brick_cube.astype(jnp.float32), gain_one).astype(jnp.bfloat16)

    def activate_two(brick_cube):
        return pre_act(brick_cube.astype(jnp.float32), gain_two).astype(jnp.bfloat16)
    acts_one = lax.map(activate_one, cubes_in)
    halos_one = gather_halos(acts_one.reshape(flat_shape), source_brick, source_face, has_source).reshape(halo_shape)

    def hidden_one(members):
        brick_cube, halo_slabs = members
        conv_rows = convolve(pad_cube(brick_cube, halo_slabs), weight_one)
        return conv_rows.reshape(brick_cube.shape).astype(jnp.bfloat16)
    hidden = lax.map(hidden_one, (acts_one, halos_one))
    acts_two = lax.map(activate_two, hidden)
    halos_two = gather_halos(acts_two.reshape(flat_shape), source_brick, source_face, has_source).reshape(halo_shape)

    def finish_one(members):
        brick_cube, halo_slabs, input_cube, alive_rows = members
        branch = convolve(pad_cube(brick_cube, halo_slabs), weight_two).reshape(brick_cube.shape)
        masked_sum = jnp.where(alive_rows[:, None, None, None, None], input_cube.astype(jnp.float32) + branch, jnp.zeros(branch.shape, jnp.float32))
        return masked_sum.astype(jnp.bfloat16)
    output = lax.map(finish_one, (acts_two, halos_two, cubes_in, alive_mask))
    grad_rows = jnp.where(alive_mask[:, :, None, None, None, None], cot_cubes, jnp.zeros_like(cot_cubes))
    zero_weights = jnp.zeros((len(OFFSETS), channels, channels), jnp.float32)
    zero_gain = jnp.zeros((channels,), jnp.float32)

    def back_two(running, members):
        brick_cube, halo_slabs, grad_cube = members
        weight_grad, interior, halo_grad = conv_back(pad_cube(brick_cube, halo_slabs), grad_cube.reshape(-1, channels), weight_two)
        return (running + weight_grad, (interior, halo_grad))
    weight_grad_two, (inner_two, halo_grad_two) = lax.scan(back_two, zero_weights, (acts_two, halos_two, grad_rows))
    returned_two = return_grads(halo_grad_two.reshape(total_bricks, 6, edge_len * edge_len, channels), source_brick, source_face, has_source).reshape(halo_shape)

    def norm_two(running, members):
        hidden_cube, interior, returned = members
        upstream = add_faces(interior, returned)
        grad_hidden, grad_gain = pre_back(hidden_cube, gain_two, upstream)
        return (running + grad_gain, grad_hidden.astype(jnp.bfloat16))
    gain_grad_two, grad_hidden = lax.scan(norm_two, zero_gain, (hidden, inner_two, returned_two))

    def back_one(running, members):
        brick_cube, halo_slabs, grad_cube = members
        weight_grad, interior, halo_grad = conv_back(pad_cube(brick_cube, halo_slabs), grad_cube.reshape(-1, channels), weight_one)
        return (running + weight_grad, (interior, halo_grad))
    weight_grad_one, (inner_one, halo_grad_one) = lax.scan(back_one, zero_weights, (acts_one, halos_one, grad_hidden))
    returned_one = return_grads(halo_grad_one.reshape(total_bricks, 6, edge_len * edge_len, channels), source_brick, source_face, has_source).reshape(halo_shape)

    def norm_one(running, members):
        input_cube, interior, returned, cot_cube, alive_rows = members
        upstream = add_faces(interior, returned)
        grad_input, grad_gain = pre_back(input_cube, gain_one, upstream)
        direct = jnp.where(alive_rows[:, None, None, None, None], cot_cube.astype(jnp.float32), jnp.zeros(grad_input.shape, jnp.float32))
        return (running + grad_gain, (direct + grad_input).astype(jnp.bfloat16))
    gain_grad_one, grad_features = lax.scan(norm_one, zero_gain, (cubes_in, inner_one, returned_one, cot_cubes, alive_mask))
    grad_scale = 1.0 / math.sqrt(SHAPES * BRICKS * VOX)
    full_shape = (SHAPES, BRICKS, VOX, channels)
    return (output.reshape(full_shape), grad_features.reshape(full_shape), weight_grad_one * grad_scale, weight_grad_two * grad_scale, gain_grad_one * grad_scale, gain_grad_two * grad_scale)
```

```python
import functools
import math

import jax
import jax.numpy as jnp
from jax import lax
from jax.experimental import pallas as pl
from jax.experimental.pallas import tpu as pltpu
from jax.sharding import PartitionSpec as P

MESH = pl.DeviceIdType.MESH
F32 = jnp.float32
BF16 = jnp.bfloat16
EPS = 1e-05
SWAP = (0, 2, 1, 4, 3, 6, 5)
XD, ZD, YD = 4, 8, 4
LO = 8


def norm(v):
    c = v - jnp.mean(v, axis=-1, keepdims=True)
    r = lax.rsqrt(jnp.mean(c * c, axis=-1, keepdims=True) + EPS)
    return c * r, r


def silu_parts(t):
    s = 1.0 / (1.0 + jnp.exp(-t))
    return t * s, s * (1.0 + t * (1.0 - s))


def rounded(v):
    return v.astype(BF16).astype(F32)


def dot(a, b):
    return jnp.dot(a, b, preferred_element_type=F32)


def dot_t(a, b):
    return lax.dot_general(a, b, (((0,), (0,)), ((), ())), preferred_element_type=F32)


def kernel(
    scale,
    send_s,
    recv_s,
    live_s,
    x_ref,
    g1_ref,
    w1_ref,
    g2_ref,
    w2_ref,
    cot_ref,
    out_ref,
    gf_ref,
    gw1_ref,
    gw2_ref,
    gg1_ref,
    gg2_ref,
    *scratch,
):
    gath = [scratch[i * 8 : i * 8 + 8] for i in range(4)]
    inb = scratch[32:36]
    (
    outb,
    tbl,
    a32,
    s32,
    u7,
    v7,
    hid,
    act2,
    acc,
    acc2,
    hal,
    hald,
    ret,
    wt1,
    wt2,
    wg,
    fin,
    ac_out,
    ac_in,
    ay_out,
    ay_in,
    ax_out,
    ax_in,
    az,
    ring_send,
    ring_recv,
    x_send,
    x_recv,
    t_sem,
    ar_sem,
    ag_sem,
    ) = scratch[36:]
    y = lax.axis_index("shape")
    sp = lax.axis_index("space")
    xi = sp // 16
    zi = (sp // 2) % ZD
    ci = sp % 2

    def dev(yy, xx, zz, cc):
        return (yy, (xx * ZD + zz) * 2 + cc)

    def z_dev(o):
        return dev(y, xi, (zi + o) % ZD, ci)

    def row_dev(l):
        return dev(y, (xi + l // 2) % XD, zi, (ci + l % 2) % 2)

    def x_dev(o):
        return dev(y, (xi + o) % XD, zi, ci)

    def y_dev(o):
        return dev((y + o) % YD, xi, zi, ci)

    sibling = dev(y, xi, zi, 1 - ci)

    barrier = pltpu.get_barrier_semaphore()
    for o in range(1, ZD):
        pl.semaphore_signal(barrier, inc=1, device_id=z_dev(o), device_id_type=MESH)
    for l in range(1, 8):
        pl.semaphore_signal(barrier, inc=1, device_id=row_dev(l), device_id_type=MESH)
    for o in range(1, YD):
        pl.semaphore_signal(barrier, inc=1, device_id=y_dev(o), device_id_type=MESH)

    def push(src, dst, ssem, rsem, target):
        pltpu.make_async_remote_copy(
            src_ref=src,
            dst_ref=dst,
            send_sem=ssem,
            recv_sem=rsem,
            device_id=target,
            device_id_type=MESH,
        ).start()

    def wait(ref, sem):
        pltpu.make_async_copy(ref, ref, sem).wait()

    def ring(pay, src, dst, b, step):
        push(
            gath[pay][src].at[pl.ds(b * 6, 6)],
            gath[pay][dst].at[pl.ds(b * 6, 6)],
            ring_send.at[pay, dst, b],
            ring_recv.at[pay, dst, b],
            z_dev(step),
        )

    def ring_wait(pay, slot, b):
        wait(gath[pay][slot].at[pl.ds(b * 6, 6)], ring_recv.at[pay, slot, b])

    def forward(pay, h):
        if h == 0:
            for b in range(2):
                ring(pay, 0, 1, b, 1)
                ring(pay, 0, ZD - 1, b, ZD - 1)
        elif h < 4:
            for b in range(2):
                ring_wait(pay, h, b)
                if h < 3 or b == 0:
                    ring(pay, h, h + 1, b, 1)
            for b in range(2):
                ring_wait(pay, ZD - h, b)
                if h < 3 or b == 1:
                    ring(pay, ZD - h, ZD - 1 - h, b, ZD - 1)
        else:
            ring_wait(pay, 4, 0)
            ring_wait(pay, 4, 1)

    def select(pay, o):
        row = tbl[o, pl.ds(o, 1), :]
        for l in range(8):
            lane = l + 8 * (pay % 2)
            code = jnp.maximum(row[0, lane], 0)
            slab = gath[pay][o][code]
            if l == 0:
                inb[pay][o * 8] = slab
            else:
                outb[pay, o, l] = slab
                push(
                    outb.at[pay, o, l],
                    inb[pay].at[o * 8 + l],
                    x_send.at[pay, o],
                    x_recv.at[pay, o],
                    row_dev(l),
                )

    def arrived(pay, o):
        wait(inb[pay].at[pl.ds(o * 8 + 1, 7)], x_recv.at[pay, o])

    def hop(pay, h):
        forward(pay, h)
        select(pay, h)
        if 0 < h < 4:
            select(pay, ZD - h)

    def add_returns(pay, o, first):
        codes = []
        for l in range(8):
            r = ((xi - l // 2 + XD) % XD * ZD + (zi - o + ZD) % ZD) * 2 + (ci + l % 2) % 2
            codes.append(send_s[r])

        def one(q, carry):
            total = jnp.zeros((64, 128), F32) if first else ret[q]
            for l in range(8):
                m = (codes[l] == q).astype(F32)
                total = total + inb[pay][o * 8 + l].astype(F32) * m
            ret[q] = total
            return carry

        lax.fori_loop(0, 12, one, 0)

    def take_halo(pay, q):
        r = recv_s[q]
        p = jnp.maximum(r, 0)
        idx = ((zi - (p // 2) % ZD + ZD) % ZD) * 8 + ((xi - p // 16 + XD) % XD) * 2 + (ci + p % 2) % 2
        return inb[pay][idx].astype(F32) * (r >= 0).astype(F32)

    def chunks(n, size, body):
        def step(i, carry):
            body(pl.multiple_of(i * size, size))
            return carry

        lax.fori_loop(0, n, step, 0)

    def faces(pay):
        for n in range(2):
            base = LO + n * 512
            cube = a32[pl.ds(base, 512), :].reshape(8, 8, 8, 128)
            gath[pay][0][n * 6] = a32[pl.ds(base, 64), :].astype(BF16)
            gath[pay][0][n * 6 + 1] = a32[pl.ds(base + 448, 64), :].astype(BF16)
            gath[pay][0][n * 6 + 2] = cube[:, 0].reshape(64, 128).astype(BF16)
            gath[pay][0][n * 6 + 3] = cube[:, 7].reshape(64, 128).astype(BF16)
            gath[pay][0][n * 6 + 4] = a32[pl.ds(base, 64, stride=8), :].astype(BF16)
            gath[pay][0][n * 6 + 5] = a32[pl.ds(base + 7, 64, stride=8), :].astype(BF16)

    def columns(dst, halo):
        for n in range(2):
            base = LO + n * 512
            rows = pl.ds(n * 512, 512)

            def h(f):
                return jnp.zeros((64, 128), F32) if halo is None else halo[n * 6 + f]

            body = a32[pl.ds(base, 512), :]
            half = body.astype(BF16)
            dst[rows, 0:128] = half
            dst[pl.ds(n * 512, 64), 128:256] = h(0).astype(BF16)
            dst[pl.ds(n * 512 + 64, 448), 128:256] = half[:448]
            dst[pl.ds(n * 512, 448), 256:384] = half[64:]
            dst[pl.ds(n * 512 + 448, 64), 256:384] = h(1).astype(BF16)
            cube = body.reshape(8, 8, 8, 128)
            low = jnp.concatenate([h(2).reshape(8, 1, 8, 128), cube[:, :7]], axis=1)
            dst[rows, 384:512] = low.reshape(512, 128).astype(BF16)
            high = jnp.concatenate([cube[:, 1:], h(3).reshape(8, 1, 8, 128)], axis=1)
            dst[rows, 512:640] = high.reshape(512, 128).astype(BF16)
            s32[...] = a32[pl.ds(base - 1, 512), :]
            s32[pl.ds(0, 64, stride=8), :] = h(4)
            dst[rows, 640:768] = s32[...].astype(BF16)
            s32[...] = a32[pl.ds(base + 1, 512), :]
            s32[pl.ds(7, 64, stride=8), :] = h(5)
            dst[rows, 768:896] = s32[...].astype(BF16)

    def add_face(target, n, f, term):
        base = n * 512
        if f == 0:
            target[pl.ds(base, 64), :] += term
        elif f == 1:
            target[pl.ds(base + 448, 64), :] += term
        elif f < 4:
            for i in range(8):
                target[pl.ds(base + i * 64 + (f - 2) * 56, 8), :] += term[i * 8 : i * 8 + 8]
        else:
            rows = pl.ds(base + (f - 4) * 7, 64, stride=8)
            target[rows, :] = target[rows, :] + term

    gain1 = g1_ref[...]
    gain2 = g2_ref[...]
    alive = [live_s[n].astype(F32) for n in range(2)]

    a32[pl.ds(LO, 1024), :] = x_ref[...].astype(F32)
    faces(0)
    step_id = lax.broadcasted_iota(jnp.int32, (8, 128), 0)
    lane_id = lax.broadcasted_iota(jnp.int32, (8, 128), 1)
    in_x = lane_id % 8
    target_id = (
        ((xi + in_x // 2) % XD) * (2 * ZD) + ((zi + step_id) % ZD) * 2 + (ci + in_x % 2) % 2
    )
    codes = jnp.full((8, 128), -1, jnp.int32)
    for e in range(64):
        codes = jnp.where(target_id == e, send_s[e], codes)
    back = jnp.full((8, 128), -1, jnp.int32)
    for q in range(12):
        back = jnp.where(target_id == recv_s[q], q, back)
    tbl[0] = jnp.where(lane_id < 8, codes, back)

    pl.semaphore_wait(barrier, 17)
    for o in range(1, ZD):
        push(tbl.at[0], tbl.at[o], t_sem.at[0], t_sem.at[1], z_dev(o))
    forward(0, 0)

    for n in range(2):
        a32[pl.ds(LO + n * 512, 512), :] = cot_ref[pl.ds(n * 512, 512), :].astype(F32) * alive[n]
    faces(1)
    forward(1, 0)
    select(0, 0)
    select(1, 0)
    for t in range(7):
        src = pl.ds(SWAP[t] * 128, 128)
        wt1[pl.ds(t * 128, 128), :] = w1_ref[src, :].astype(F32).T.astype(BF16)
        wt2[pl.ds(t * 128, 128), :] = w2_ref[src, :].astype(F32).T.astype(BF16)

    wait(tbl.at[pl.ds(1, 7)], t_sem.at[1])
    for h in range(1, 5):
        hop(0, h)
        hop(1, h)
    for o in range(8):
        arrived(0, o)

    def halo_one(q, carry):
        xhat, _ = norm(take_halo(0, q))
        act, slope = silu_parts(xhat * gain1)
        hal[q] = rounded(act)
        hald[q] = slope * xhat
        return carry

    lax.fori_loop(0, 12, halo_one, 0)

    def act_one(r):
        xhat, _ = norm(x_ref[pl.ds(r, 128), :].astype(F32))
        a32[pl.ds(LO + r, 128), :] = rounded(silu_parts(xhat * gain1)[0])

    chunks(8, 128, act_one)
    columns(u7, hal)

    def hidden_rows(r):
        rows = pl.ds(r, 256)
        h = dot(u7[rows, :], w1_ref[...]).astype(BF16)
        hid[rows, :] = h
        xhat, _ = norm(h.astype(F32))
        a = silu_parts(xhat * gain2)[0].astype(BF16)
        act2[rows, :] = a
        a32[pl.ds(LO + r, 256), :] = a.astype(F32)

    chunks(4, 256, hidden_rows)
    faces(2)
    forward(2, 0)
    select(2, 0)

    for o in range(8):
        arrived(1, o)
        add_returns(1, o, o == 0)
    for n in range(2):
        a32[pl.ds(LO + n * 512, 512), :] = cot_ref[pl.ds(n * 512, 512), :].astype(F32) * alive[n]
    columns(v7, ret)

    wg[pl.ds(1792, 256), :] = jnp.zeros((256, 128), F32)

    def pre_back(v, gain, upstream):
        xhat, r = norm(v)
        _, slope = silu_parts(xhat * gain)
        dt = upstream * slope
        d = dt * gain
        mean_d = jnp.mean(d, axis=-1, keepdims=True)
        mean_dx = jnp.mean(d * xhat, axis=-1, keepdims=True)
        return r * (d - mean_d - xhat * mean_dx), dt * xhat

    def grad_hidden_rows(r):
        up = dot(v7[pl.ds(r, 256), :], wt2[...])
        grad, per = pre_back(hid[pl.ds(r, 256), :].astype(F32), gain2, up)
        a32[pl.ds(LO + r, 256), :] = rounded(grad)
        wg[pl.ds(1793, 1), :] += jnp.sum(per, axis=0, keepdims=True)

    chunks(4, 256, grad_hidden_rows)
    faces(3)
    forward(3, 0)
    select(3, 0)

    a2 = act2[...]
    for t in range(7):
        wg[pl.ds(896 + SWAP[t] * 128, 128), :] = dot_t(a2, v7[:, t * 128 : t * 128 + 128])
    gh = a32[pl.ds(LO, 1024), :].astype(BF16)
    for t in range(7):
        wg[pl.ds(t * 128, 128), :] = dot_t(u7[:, t * 128 : t * 128 + 128], gh)

    columns(v7, None)

    def inner_one(r):
        rows = pl.ds(r, 256)
        up = dot(v7[rows, :], wt1[...])
        acc2[rows, :] = up
        xhat, _ = norm(x_ref[rows, :].astype(F32))
        slope = silu_parts(xhat * gain1)[1]
        wg[pl.ds(1792, 1), :] += jnp.sum(up * slope * xhat, axis=0, keepdims=True)

    chunks(4, 256, inner_one)
    for f in range(6):
        w = wt1[pl.ds(SWAP[f + 1] * 128, 128), :]
        for n in range(2):
            q = n * 6 + f
            term = rounded(dot(gath[3][0][q], w)) * hald[q]
            wg[pl.ds(1792, 1), :] += jnp.sum(term, axis=0, keepdims=True)

    mine = pl.multiple_of(ci * 1024, 1024)
    other = pl.multiple_of((1 - ci) * 1024, 1024)
    ac_out[...] = wg[pl.ds(other, 1024), :].astype(BF16)
    push(ac_out, ac_in, ar_sem.at[0, 0], ar_sem.at[0, 1], sibling)

    hop(2, 1)
    hop(3, 1)

    wait(ac_in, ar_sem.at[0, 1])
    wg[pl.ds(mine, 1024), :] += ac_in[...].astype(F32)
    for o in range(1, YD):
        start = pl.multiple_of(mine + ((y + o) % YD) * 256, 256)
        ay_out[o] = wg[pl.ds(start, 256), :].astype(BF16)
        push(ay_out.at[o], ay_in.at[o], ar_sem.at[1, 0], ar_sem.at[1, 1], y_dev(o))

    hop(2, 2)
    hop(3, 2)

    a32[pl.ds(LO, 1024), :] = act2[...].astype(F32)
    columns(u7, None)

    def inner_two(r):
        rows = pl.ds(r, 256)
        acc[rows, :] = dot(u7[rows, :], w2_ref[...])

    chunks(4, 256, inner_two)

    wait(ay_in.at[pl.ds(1, 3)], ar_sem.at[1, 1])
    mine_y = pl.multiple_of(mine + y * 256, 256)
    part = wg[pl.ds(mine_y, 256), :]
    for o in range(1, YD):
        part = part + ay_in[o].astype(F32)
    wg[pl.ds(mine_y, 256), :] = part
    for o in range(1, XD):
        start = pl.multiple_of(mine_y + ((xi + o) % XD) * 64, 64)
        ax_out[o] = wg[pl.ds(start, 64), :].astype(BF16)
        push(ax_out.at[o], ax_in.at[o], ar_sem.at[2, 0], ar_sem.at[2, 1], x_dev(o))

    hop(2, 3)
    hop(3, 3)

    wait(ax_in.at[pl.ds(1, 3)], ar_sem.at[2, 1])
    mine_x = pl.multiple_of(mine_y + xi * 64, 64)
    part = wg[pl.ds(mine_x, 64), :]
    for o in range(1, XD):
        part = part + ax_in[o].astype(F32)
    az[0] = part.astype(BF16)
    for o in range(1, ZD):
        push(az.at[0], az.at[o], ar_sem.at[3, 0], ar_sem.at[3, 1], z_dev(o))

    hop(2, 4)
    hop(3, 4)

    wait(az.at[pl.ds(1, 7)], ar_sem.at[3, 1])
    total = jnp.zeros((64, 128), F32)
    for k in range(ZD):
        total = total + az[(zi - k + ZD) % ZD].astype(F32)
    fin[pl.ds(mine_x, 64), :] = total * scale
    piece = fin.at[pl.ds(mine_x, 64)]
    for o in range(1, XD):
        push(piece, piece, ag_sem.at[0, 0, o], ag_sem.at[0, 1, o], x_dev(o))

    for o in range(8):
        arrived(2, o)
    for f in range(6):
        w = w2_ref[pl.ds((f + 1) * 128, 128), :]
        for n in range(2):
            add_face(acc, n, f, dot(take_halo(2, n * 6 + f).astype(BF16), w))
    for n in range(2):
        rows = pl.ds(n * 512, 512)
        out_ref[rows, :] = ((x_ref[rows, :].astype(F32) + acc[rows, :]) * alive[n]).astype(BF16)

    for o in range(1, XD):
        start = pl.multiple_of(mine_y + ((xi - o + XD) % XD) * 64, 64)
        wait(fin.at[pl.ds(start, 64)], ag_sem.at[0, 1, o])
    piece = fin.at[pl.ds(mine_y, 256)]
    for o in range(1, YD):
        push(piece, piece, ag_sem.at[1, 0, o], ag_sem.at[1, 1, o], y_dev(o))

    for o in range(8):
        arrived(3, o)
        add_returns(3, o, o == 0)
    for f in range(6):
        w = wt1[pl.ds((f + 1) * 128, 128), :]
        for n in range(2):
            add_face(acc2, n, f, dot(ret[n * 6 + f].astype(BF16), w))
    for n in range(2):

        def grad_rows(r, n=n):
            rows = pl.ds(n * 512 + r, 256)
            grad, _ = pre_back(x_ref[rows, :].astype(F32), gain1, acc2[rows, :])
            gf_ref[rows, :] = (cot_ref[rows, :].astype(F32) * alive[n] + grad).astype(BF16)

        chunks(2, 256, grad_rows)

    for o in range(1, YD):
        start = pl.multiple_of(mine + ((y - o + YD) % YD) * 256, 256)
        wait(fin.at[pl.ds(start, 256)], ag_sem.at[1, 1, o])
    piece = fin.at[pl.ds(mine, 1024)]
    push(piece, piece, ag_sem.at[2, 0, 0], ag_sem.at[2, 1, 0], sibling)
    wait(fin.at[pl.ds(other, 1024)], ag_sem.at[2, 1, 0])
    gw1_ref[...] = fin[pl.ds(0, 896), :]
    gw2_ref[...] = fin[pl.ds(896, 896), :]
    gg1_ref[...] = fin[pl.ds(1792, 1), :]
    gg2_ref[...] = fin[pl.ds(1793, 1), :]

    for pay in range(4):
        for o in range(1, ZD):
            for b in range(2):
                wait(gath[pay][o].at[pl.ds(b * 6, 6)], ring_send.at[pay, o, b])
        for o in range(ZD):
            wait(outb.at[pay, o, pl.ds(1, 7)], x_send.at[pay, o])
    wait(tbl.at[pl.ds(1, 7)], t_sem.at[0])
    wait(ac_out, ar_sem.at[0, 0])
    wait(ay_out.at[pl.ds(1, 3)], ar_sem.at[1, 0])
    wait(ax_out.at[pl.ds(1, 3)], ar_sem.at[2, 0])
    wait(az.at[pl.ds(1, 7)], ar_sem.at[3, 0])
    for o in range(1, XD):
        wait(fin.at[pl.ds(mine_x, 64)], ag_sem.at[0, 0, o])
        wait(fin.at[pl.ds(mine_y, 256)], ag_sem.at[1, 0, o])
    wait(fin.at[pl.ds(mine, 1024)], ag_sem.at[2, 0, 0])


def shards(
    features, gain_one, weight_one, gain_two, weight_two, live, send_index, recv_index, cotangent
):
    scale = 1.0 / math.sqrt(
        features.shape[1] * features.shape[2] * lax.axis_size("shape") * lax.axis_size("space")
    )
    rows = 1024
    smem = pl.BlockSpec(memory_space=pltpu.SMEM)
    vmem = pl.BlockSpec(memory_space=pltpu.VMEM)
    results = pl.pallas_call(
        functools.partial(kernel, scale),
        out_shape=[
            jax.ShapeDtypeStruct((rows, 128), BF16),
            jax.ShapeDtypeStruct((rows, 128), BF16),
            jax.ShapeDtypeStruct((896, 128), F32),
            jax.ShapeDtypeStruct((896, 128), F32),
            jax.ShapeDtypeStruct((1, 128), F32),
            jax.ShapeDtypeStruct((1, 128), F32),
        ],
        in_specs=[smem] * 3 + [vmem] * 6,
        out_specs=[vmem] * 6,
        scratch_shapes=[
            *[pltpu.VMEM((12, 64, 128), BF16)] * 32,
            *[pltpu.VMEM((64, 64, 128), BF16)] * 4,
            pltpu.VMEM((4, 8, 8, 64, 128), BF16),
            pltpu.VMEM((8, 8, 128), jnp.int32),
            pltpu.VMEM((1040, 128), F32),
            pltpu.VMEM((512, 128), F32),
            pltpu.VMEM((rows, 896), BF16),
            pltpu.VMEM((rows, 896), BF16),
            pltpu.VMEM((rows, 128), BF16),
            pltpu.VMEM((rows, 128), BF16),
            pltpu.VMEM((rows, 128), F32),
            pltpu.VMEM((rows, 128), F32),
            pltpu.VMEM((12, 64, 128), F32),
            pltpu.VMEM((12, 64, 128), F32),
            pltpu.VMEM((12, 64, 128), F32),
            pltpu.VMEM((896, 128), BF16),
            pltpu.VMEM((896, 128), BF16),
            pltpu.VMEM((2048, 128), F32),
            pltpu.VMEM((2048, 128), F32),
            pltpu.VMEM((1024, 128), BF16),
            pltpu.VMEM((1024, 128), BF16),
            pltpu.VMEM((4, 256, 128), BF16),
            pltpu.VMEM((4, 256, 128), BF16),
            pltpu.VMEM((4, 64, 128), BF16),
            pltpu.VMEM((4, 64, 128), BF16),
            pltpu.VMEM((8, 64, 128), BF16),
            pltpu.SemaphoreType.DMA((4, 8, 2)),
            pltpu.SemaphoreType.DMA((4, 8, 2)),
            pltpu.SemaphoreType.DMA((4, 8)),
            pltpu.SemaphoreType.DMA((4, 8)),
            pltpu.SemaphoreType.DMA((2,)),
            pltpu.SemaphoreType.DMA((4, 2)),
            pltpu.SemaphoreType.DMA((3, 2, 4)),
        ],
        compiler_params=pltpu.CompilerParams(
            collective_id=0, has_side_effects=True, vmem_limit_bytes=48 * 1024 * 1024
        ),
    )(
        send_index.reshape(64),
        recv_index.reshape(12),
        live.reshape(2),
        features.reshape(rows, 128),
        gain_one.reshape(1, 128),
        weight_one.reshape(896, 128),
        gain_two.reshape(1, 128),
        weight_two.reshape(896, 128),
        cotangent.reshape(rows, 128),
    )
    out, grad, w1, w2, g1, g2 = results
    return (
        out.reshape(features.shape),
        grad.reshape(features.shape),
        w1.reshape(7, 128, 128),
        w2.reshape(7, 128, 128),
        g1.reshape(128),
        g2.reshape(128),
    )


def solution(mesh):
    bricks = P("shape", "space", None, None)
    in_specs = (
        bricks,
        P(),
        P(),
        P(),
        P(),
        P("shape", "space"),
        bricks,
        P("shape", "space", None),
        bricks,
    )
    out_specs = (bricks, bricks, P(), P(), P(), P())
    return jax.shard_map(shards, mesh=mesh, in_specs=in_specs, out_specs=out_specs, check_vma=False)
```

```python
import functools
import math

import jax
import jax.numpy as jnp
from jax import lax
from jax.experimental import pallas as pl
from jax.experimental.pallas import tpu as pltpu
from jax.sharding import PartitionSpec as P

MESH = pl.DeviceIdType.MESH
F32 = jnp.float32
BF16 = jnp.bfloat16
EPS = 1e-05
SWAP = (0, 2, 1, 4, 3, 6, 5)
XD, ZD, YD = 4, 8, 4
LO = 8
POS = (0, 1, 3, 5, 7, 6, 4, 2)
GROUPS = ((0, 3), (3, 2), (5, 2), (7, 1))


def norm(v):
    c = v - jnp.mean(v, axis=-1, keepdims=True)
    r = lax.rsqrt(jnp.mean(c * c, axis=-1, keepdims=True) + EPS)
    return c * r, r


def silu_parts(t):
    s = 1.0 / (1.0 + jnp.exp(-t))
    return t * s, s * (1.0 + t * (1.0 - s))


def rounded(v):
    return v.astype(BF16).astype(F32)


def dot(a, b):
    return jnp.dot(a, b, preferred_element_type=F32)


def dot_t(a, b):
    return lax.dot_general(a, b, (((0,), (0,)), ((), ())), preferred_element_type=F32)


def kernel(
    scale,
    send_s,
    recv_s,
    live_s,
    x_hbm,
    g1_hbm,
    w1_hbm,
    g2_hbm,
    w2_hbm,
    cot_hbm,
    out_hbm,
    gf_hbm,
    gw1_hbm,
    gw2_hbm,
    gg1_hbm,
    gg2_hbm,
    *scratch,
):
    gath = [scratch[i * 8 : i * 8 + 8] for i in range(4)]
    inb = scratch[32:36]
    (
        outb,
        tbl,
        tbl_s,
        ordv,
        ord_s,
        seg,
        col,
        fout,
        x_ref,
        cot_ref,
        w1_ref,
        w2_ref,
        gains,
        out_ref,
        gf_ref,
        a32,
        s32,
        e32,
        u7,
        v7,
        act2,
        acc,
        acc2,
        xh1,
        sl1,
        rs1,
        xh2,
        sl2,
        rs2,
        hal,
        hald,
        ret,
        wt1,
        wt2,
        wg,
        fin,
        ay_out,
        ay_in,
        ax_out,
        ax_in,
        az,
        ring_send,
        ring_recv,
        x_send,
        x_recv,
        t_sem,
        ar_sem,
        ag_sem,
        ld_sem,
        st_sem,
    ) = scratch[36:]
    y = lax.axis_index("shape")
    sp = lax.axis_index("space")
    xi = sp // 16
    zi = (sp // 2) % ZD
    ci = sp % 2

    def dev(yy, xx, zz, cc):
        return (yy, (xx * ZD + zz) * 2 + cc)

    def z_dev(o):
        return dev(y, xi, (zi + o) % ZD, ci)

    def row_dev(l, step=0):
        return dev(y, (xi + l // 2) % XD, (zi + step + ZD) % ZD, (ci + l % 2) % 2)

    def row_source(l, step):
        return dev(y, (xi - l // 2 + XD) % XD, (zi + step + ZD) % ZD, (ci + l % 2) % 2)

    def x_dev(o):
        return dev(y, (xi + o) % XD, zi, ci)

    def y_dev(j):
        return dev((y + j // 2) % YD, xi, zi, (ci + j % 2) % 2)

    barrier = pltpu.get_barrier_semaphore()

    def greet(target):
        pl.semaphore_signal(barrier, inc=1, device_id=target, device_id_type=MESH)

    for o in range(1, ZD):
        greet(z_dev(o))
    for l in range(1, 8):
        greet(row_dev(l))
    for j in range(2, 8):
        greet(y_dev(j))
    for l in range(1, 4):
        greet(row_source(l, -1))
    for l in range(4, 8):
        greet(row_source(l, 1))

    def load(src, dst, i):
        pltpu.make_async_copy(src, dst, ld_sem.at[i]).start()

    load(x_hbm, x_ref, 0)
    load(cot_hbm, cot_ref, 1)
    load(w1_hbm, w1_ref, 2)
    load(w2_hbm, w2_ref, 3)
    load(g1_hbm, gains.at[0], 4)
    load(g2_hbm, gains.at[1], 5)

    def push(src, dst, ssem, rsem, target):
        pltpu.make_async_remote_copy(
            src_ref=src,
            dst_ref=dst,
            send_sem=ssem,
            recv_sem=rsem,
            device_id=target,
            device_id_type=MESH,
        ).start()

    def wait(ref, sem):
        pltpu.make_async_copy(ref, ref, sem).wait()

    def part(pay, slot, k):
        if k == 0:
            return gath[pay][slot].at[:, pl.ds(0, 2)]
        return gath[pay][slot].at[:, pl.ds(2, 4), pl.ds(0, 48)]

    def ring(pay, src, dst, k, step):
        push(
            part(pay, src, k),
            part(pay, dst, k),
            ring_send.at[pay, dst, k],
            ring_recv.at[pay, dst, k],
            z_dev(step),
        )

    def forward(pay, h):
        for k in range(2):
            for src, dst, step in ((h, h + 1, 1), ((ZD - h) % ZD, ZD - 1 - h, ZD - 1)):
                if h > 0:
                    wait(part(pay, src, k), ring_recv.at[pay, src, k])
                if h < 3:
                    ring(pay, src, dst, k, step)

    def fill(pay, slot):
        g = gath[pay][slot]
        for n in range(2):
            e32[...] = g[n, 0:2].reshape(128, 128).astype(F32)
            g[n, 2, 48:64] = jnp.concatenate([e32[0:8], e32[64:72]], axis=0).astype(BF16)
            g[n, 3, 48:64] = jnp.concatenate([e32[56:64], e32[120:128]], axis=0).astype(BF16)
            g[n, 4, 48:64] = e32[pl.ds(0, 16, stride=8), :].astype(BF16)
            g[n, 5, 48:64] = e32[pl.ds(7, 16, stride=8), :].astype(BF16)

    def pick(pay, slot, o, l):
        code = jnp.maximum(tbl_s[slot, o, l + 8 * (pay % 2)], 0)
        slab = gath[pay][slot][code // 8, code % 8]
        if l == 0 and o == slot:
            inb[pay][0, POS[o]] = slab
        else:
            outb[pay, l, POS[o]] = slab

    def deliver(pay, group, l, step):
        first, count = GROUPS[group]
        push(
            outb.at[pay, l, pl.ds(first, count)],
            inb[pay].at[l, pl.ds(first, count)],
            x_send.at[pay, group],
            x_recv.at[pay, group],
            row_dev(l, step),
        )

    def select(pay, h):
        if h == 3:
            for l in range(4):
                pick(pay, 3, 4, l)
                deliver(pay, 3, l, 1)
            for l in range(4, 8):
                pick(pay, 5, 4, l)
                deliver(pay, 3, l, -1)
        for l in (4, 5, 2, 3, 6, 7, 1, 0):
            for o in ((0, 1, 7), (2, 6), (3, 5))[h - 1]:
                pick(pay, o, o, l)
            if l > 0:
                deliver(pay, h - 1, l, 0)

    def flying(group):
        first, count = GROUPS[group]
        return (pl.ds(0, 8) if group == 3 else pl.ds(1, 7)), pl.ds(first, count)

    def arrived(pay):
        for group in range(4):
            wait(inb[pay].at[flying(group)], x_recv.at[pay, group])

    def hop(pay, h):
        forward(pay, h)
        if h > 0:
            fill(pay, h)
            fill(pay, ZD - h)
            select(pay, h)

    def returns(pay):
        arrived(pay)

        def one(k, carry):
            total, before = carry
            v = ord_s[k, 0]
            code, at = v // 64, v % 64
            total = total * (code == before).astype(F32) + inb[pay][at // 8, at % 8].astype(F32)
            seg[k] = total
            return total, code

        lax.fori_loop(0, 64, one, (jnp.zeros((64, 128), F32), jnp.int32(-1)))

        def pickup(q, carry):
            start, end = ord_s[64 + q, 0], ord_s[65 + q, 0]
            ret[q] = seg[jnp.maximum(end - 1, 0)] * (end > start).astype(F32)
            return carry

        lax.fori_loop(0, 12, pickup, 0)

    def position(r):
        o = (zi - (r // 2) % ZD + ZD) % ZD
        l = ((xi - r // 16 + XD) % XD) * 2 + (ci + r % 2) % 2
        near = jnp.where(o < 4, jnp.maximum(2 * o - 1, 0), jnp.where(o > 4, 16 - 2 * o, 7))
        return l * 8 + near

    def take_halo(pay, q):
        r = recv_s[q // 6, q % 6]
        at = position(jnp.maximum(r, 0))
        return inb[pay][at // 8, at % 8].astype(F32) * (r >= 0).astype(F32)

    def chunks(n, size, body):
        def step(i, carry):
            body(pl.multiple_of(i * size, size))
            return carry

        lax.fori_loop(0, n, step, 0)

    def ordered(v):
        v = v.reshape(8, 8, 128)
        return jnp.concatenate([v[1:7], v[0:1], v[7:8]], axis=0).reshape(64, 128)

    def natural(v):
        v = v.reshape(8, 8, 128)
        return jnp.concatenate([v[6:7], v[0:6], v[7:8]], axis=0).reshape(64, 128)

    def faces(pay):
        g = gath[pay][0]
        for n in range(2):
            base = LO + n * 512
            cube = a32[pl.ds(base, 512), :].reshape(8, 8, 8, 128)
            g[n, 0] = a32[pl.ds(base, 64), :].astype(BF16)
            g[n, 1] = a32[pl.ds(base + 448, 64), :].astype(BF16)
            g[n, 2] = ordered(cube[:, 0]).astype(BF16)
            g[n, 3] = ordered(cube[:, 7]).astype(BF16)
            g[n, 4] = ordered(a32[pl.ds(base, 64, stride=8), :]).astype(BF16)
            g[n, 5] = ordered(a32[pl.ds(base + 7, 64, stride=8), :]).astype(BF16)

    def columns(dst):
        zero = jnp.zeros((64, 128), F32)
        plate = jnp.zeros((8, 1, 8, 128), F32)
        for n in range(2):
            base = LO + n * 512
            rows = pl.ds(n * 512, 512)
            body = a32[pl.ds(base, 512), :]
            half = body.astype(BF16)
            dst[rows, 0:128] = half
            dst[pl.ds(n * 512, 64), 128:256] = zero.astype(BF16)
            dst[pl.ds(n * 512 + 64, 448), 128:256] = half[:448]
            dst[pl.ds(n * 512, 448), 256:384] = half[64:]
            dst[pl.ds(n * 512 + 448, 64), 256:384] = zero.astype(BF16)
            cube = body.reshape(8, 8, 8, 128)
            low = jnp.concatenate([plate, cube[:, :7]], axis=1)
            dst[rows, 384:512] = low.reshape(512, 128).astype(BF16)
            high = jnp.concatenate([cube[:, 1:], plate], axis=1)
            dst[rows, 512:640] = high.reshape(512, 128).astype(BF16)
            s32[...] = a32[pl.ds(base - 1, 512), :]
            s32[pl.ds(0, 64, stride=8), :] = zero
            dst[rows, 640:768] = s32[...].astype(BF16)
            s32[...] = a32[pl.ds(base + 1, 512), :]
            s32[pl.ds(7, 64, stride=8), :] = zero
            dst[rows, 768:896] = s32[...].astype(BF16)

    def add_face(target, n, f, term):
        base = n * 512
        if f == 0:
            target[pl.ds(base, 64), :] += term
        elif f == 1:
            target[pl.ds(base + 448, 64), :] += term
        elif f < 4:
            term = natural(term)
            for i in range(8):
                target[pl.ds(base + i * 64 + (f - 2) * 56, 8), :] += term[i * 8 : i * 8 + 8]
        else:
            rows = pl.ds(base + (f - 4) * 7, 64, stride=8)
            target[rows, :] = target[rows, :] + natural(term)

    def add_faces(target, slab, w):
        for f in range(6):
            both = jnp.concatenate([slab(f), slab(6 + f)], axis=0)
            term = dot(both, w[pl.ds((f + 1) * 128, 128), :])
            add_face(target, 0, f, term[:64])
            add_face(target, 1, f, term[64:])

    def product(target, cols, w):
        def rows_of(r):
            rows = pl.ds(r, 256)
            target[rows, :] = dot(cols[rows, :], w[...])

        chunks(4, 256, rows_of)

    def back_rows(r, up, gain, xh, sl, rs):
        rows = pl.ds(r, 128)
        xhat = xh[rows, :]
        dt = up * sl[rows, :]
        d = dt * gain
        mean_d = jnp.mean(d, axis=-1, keepdims=True)
        mean_dx = jnp.mean(d * xhat, axis=-1, keepdims=True)
        return rs[rows, :] * (d - mean_d - xhat * mean_dx), dt * xhat

    def pre_rows(v, r, gain, xh, sl, rs):
        rows = pl.ds(r, 128)
        xhat, inv = norm(v)
        a, slope = silu_parts(xhat * gain)
        xh[rows, :] = xhat
        sl[rows, :] = slope
        rs[rows, :] = jnp.broadcast_to(inv, (128, 128))
        return a

    alive = [live_s[n].astype(F32) for n in range(2)]

    step_id = lax.broadcasted_iota(jnp.int32, (8, 128), 0)
    lane_id = lax.broadcasted_iota(jnp.int32, (8, 128), 1)
    in_x = lane_id % 8
    target_id = (
        ((xi + in_x // 2) % XD) * (2 * ZD) + ((zi + step_id) % ZD) * 2 + (ci + in_x % 2) % 2
    )
    codes = jnp.full((8, 128), -1, jnp.int32)
    for e in range(64):
        codes = jnp.where(target_id == e, send_s[e], codes)
    back = jnp.full((8, 128), -1, jnp.int32)
    for q in range(12):
        back = jnp.where(target_id == recv_s[q // 6, q % 6], q, back)
    chosen = jnp.where(lane_id < 8, codes, back)
    tbl[0] = chosen + 2 * (chosen >= 6).astype(jnp.int32)

    wait(x_ref, ld_sem.at[0])
    a32[pl.ds(LO, 1024), :] = x_ref[...].astype(F32)
    faces(0)
    pl.semaphore_wait(barrier, 27)
    for o in range(1, ZD):
        push(tbl.at[0], tbl.at[o], t_sem.at[0], t_sem.at[1], z_dev(o))
    forward(0, 0)

    lane = lax.broadcasted_iota(jnp.int32, (64, 128), 1)
    line = lax.broadcasted_iota(jnp.int32, (64, 128), 0)
    across = jnp.full((8, 128), 99, jnp.int32)
    for e in range(64):
        across = jnp.where(lane_id == e, send_s[e], across)
        col[pl.ds(e, 1), :] = jnp.full((1, 128), send_s[e], jnp.int32)
    across = jnp.broadcast_to(across[0:1], (64, 128))
    down = col[...]
    ahead = (down < across) | ((down == across) & (line < lane))
    rank = jnp.sum(ahead.astype(jnp.int32), axis=0, keepdims=True)
    value = position(jnp.minimum(lane, 63)) + 64 * (jnp.minimum(across, 15) + 1)
    sorted_values = jnp.sum(
        jnp.where((rank == line) & (lane < 64), value, 0), axis=1, keepdims=True
    )
    ordv[pl.ds(0, 64), :] = jnp.broadcast_to(sorted_values, (64, 128))
    below = jnp.sum((across < line).astype(jnp.int32), axis=1, keepdims=True)
    ordv[pl.ds(64, 16), :] = jnp.broadcast_to(below, (64, 128))[:16]
    pltpu.make_async_copy(ordv, ord_s, ld_sem.at[7]).start()

    wait(cot_ref, ld_sem.at[1])
    for n in range(2):
        a32[pl.ds(LO + n * 512, 512), :] = cot_ref[pl.ds(n * 512, 512), :].astype(F32) * alive[n]
    faces(1)
    columns(v7)
    wait(tbl.at[pl.ds(1, 7)], t_sem.at[1])
    codes_in = pltpu.make_async_copy(tbl, tbl_s, ld_sem.at[6])
    codes_in.start()
    codes_in.wait()
    hop(0, 1)

    wait(gains.at[0], ld_sem.at[4])
    wait(gains.at[1], ld_sem.at[5])
    gain1 = gains[0]
    gain2 = gains[1]

    def act_one(r):
        a = pre_rows(x_ref[pl.ds(r, 128), :].astype(F32), r, gain1, xh1, sl1, rs1)
        a32[pl.ds(LO + r, 128), :] = rounded(a)

    chunks(8, 128, act_one)
    hop(0, 2)
    hop(1, 0)
    columns(u7)
    wait(w1_ref, ld_sem.at[2])
    wait(w2_ref, ld_sem.at[3])
    product(acc, u7, w1_ref)
    hop(0, 3)
    for t in range(7):
        src = pl.ds(SWAP[t] * 128, 128)
        wt1[pl.ds(t * 128, 128), :] = w1_ref[src, :].astype(F32).T.astype(BF16)
        wt2[pl.ds(t * 128, 128), :] = w2_ref[src, :].astype(F32).T.astype(BF16)
    product(acc2, v7, wt2)
    hop(1, 1)

    arrived(0)

    def halo_one(q, carry):
        xhat, _ = norm(take_halo(0, q))
        act, slope = silu_parts(xhat * gain1)
        hal[q] = act.astype(BF16)
        hald[q] = slope * xhat
        return carry

    lax.fori_loop(0, 12, halo_one, 0)
    add_faces(acc, lambda q: hal[q], w1_ref)

    def hidden_rows(r):
        rows = pl.ds(r, 128)
        a = pre_rows(rounded(acc[rows, :]), r, gain2, xh2, sl2, rs2).astype(BF16)
        act2[rows, :] = a
        a32[pl.ds(LO + r, 128), :] = a.astype(F32)

    chunks(8, 128, hidden_rows)
    faces(2)
    hop(1, 2)
    hop(2, 0)

    hop(1, 3)
    hop(2, 1)
    pltpu.make_async_copy(ordv, ord_s, ld_sem.at[7]).wait()
    returns(1)
    add_faces(acc2, lambda q: ret[q].astype(BF16), wt2)
    wg[pl.ds(1792, 256), :] = jnp.zeros((256, 128), F32)

    def grad_hidden_rows(r):
        grad, per = back_rows(r, acc2[pl.ds(r, 128), :], gain2, xh2, sl2, rs2)
        a32[pl.ds(LO + r, 128), :] = rounded(grad)
        wg[pl.ds(1793, 1), :] += jnp.sum(per, axis=0, keepdims=True)

    chunks(8, 128, grad_hidden_rows)
    faces(3)
    hop(3, 0)

    def slabs(pay, f):
        return gath[pay][0][:, f].reshape(128, 128)

    a2 = act2[...]
    for t in range(7):
        total = dot_t(a2, v7[:, t * 128 : t * 128 + 128])
        if t > 0:
            r2 = jnp.concatenate([ret[t - 1], ret[t + 5]], axis=0).astype(BF16)
            total = total + dot_t(slabs(2, t - 1), r2)
        wg[pl.ds(896 + SWAP[t] * 128, 128), :] = total
    hop(2, 2)
    gh = a32[pl.ds(LO, 1024), :].astype(BF16)
    for t in range(7):
        total = dot_t(u7[:, t * 128 : t * 128 + 128], gh)
        if t > 0:
            h2 = jnp.concatenate([hal[t - 1], hal[t + 5]], axis=0)
            total = total + dot_t(h2, slabs(3, t - 1))
        wg[pl.ds(t * 128, 128), :] = total

    columns(v7)
    product(acc2, v7, wt1)

    def gain_rows(r):
        rows = pl.ds(r, 128)
        per = acc2[rows, :] * sl1[rows, :] * xh1[rows, :]
        wg[pl.ds(1792, 1), :] += jnp.sum(per, axis=0, keepdims=True)

    chunks(8, 128, gain_rows)
    for f in range(6):
        both = dot(slabs(3, f), wt1[pl.ds(SWAP[f + 1] * 128, 128), :])
        slope = jnp.concatenate([hald[f], hald[6 + f]], axis=0)
        wg[pl.ds(1792, 1), :] += jnp.sum(rounded(both) * slope, axis=0, keepdims=True)

    mine = pl.multiple_of(ci * 1024 + y * 256, 256)
    for j in range(1, 8):
        start = pl.multiple_of((ci + j % 2) % 2 * 1024 + (y + j // 2) % YD * 256, 256)
        ay_out[j] = wg[pl.ds(start, 256), :].astype(BF16)
        push(ay_out.at[j], ay_in.at[j], ar_sem.at[0, 0], ar_sem.at[0, 1], y_dev(j))

    hop(3, 1)
    hop(2, 3)

    a32[pl.ds(LO, 1024), :] = act2[...].astype(F32)
    columns(u7)
    product(acc, u7, w2_ref)

    wait(ay_in.at[pl.ds(1, 7)], ar_sem.at[0, 1])
    partial = wg[pl.ds(mine, 256), :]
    for j in range(1, 8):
        partial = partial + ay_in[j].astype(F32)
    wg[pl.ds(mine, 256), :] = partial
    for o in range(1, XD):
        start = pl.multiple_of(mine + ((xi + o) % XD) * 64, 64)
        ax_out[o] = wg[pl.ds(start, 64), :].astype(BF16)
        push(ax_out.at[o], ax_in.at[o], ar_sem.at[1, 0], ar_sem.at[1, 1], x_dev(o))

    hop(3, 2)

    wait(ax_in.at[pl.ds(1, 3)], ar_sem.at[1, 1])
    mine_x = pl.multiple_of(mine + xi * 64, 64)
    partial = wg[pl.ds(mine_x, 64), :]
    for o in range(1, XD):
        partial = partial + ax_in[o].astype(F32)
    az[0] = partial.astype(BF16)
    for o in range(1, ZD):
        push(az.at[0], az.at[o], ar_sem.at[2, 0], ar_sem.at[2, 1], z_dev(o))

    arrived(2)
    add_faces(acc, lambda q: take_halo(2, q).astype(BF16), w2_ref)
    for n in range(2):
        rows = pl.ds(n * 512, 512)
        out_ref[rows, :] = ((x_ref[rows, :].astype(F32) + acc[rows, :]) * alive[n]).astype(BF16)

    def store(src, dst, i):
        pltpu.make_async_copy(src, dst, st_sem.at[i]).start()

    store(out_ref, out_hbm, 0)

    wait(az.at[pl.ds(1, 7)], ar_sem.at[2, 1])
    total = jnp.zeros((64, 128), F32)
    for k in range(ZD):
        total = total + az[(zi - k + ZD) % ZD].astype(F32)
    fin[pl.ds(mine_x, 64), :] = (total * scale).astype(BF16)
    piece = fin.at[pl.ds(mine_x, 64)]
    for o in range(1, XD):
        push(piece, piece, ag_sem.at[0, 0, o], ag_sem.at[0, 1, o], x_dev(o))

    hop(3, 3)

    for o in range(1, XD):
        start = pl.multiple_of(mine + ((xi - o + XD) % XD) * 64, 64)
        wait(fin.at[pl.ds(start, 64)], ag_sem.at[0, 1, o])
    piece = fin.at[pl.ds(mine, 256)]
    for j in range(1, 8):
        push(piece, piece, ag_sem.at[1, 0, j], ag_sem.at[1, 1, j], y_dev(j))

    returns(3)
    add_faces(acc2, lambda q: ret[q].astype(BF16), wt1)
    for n in range(2):

        def grad_rows(i, n=n):
            r = pl.multiple_of(n * 512 + i, 128)
            rows = pl.ds(r, 128)
            grad, _ = back_rows(r, acc2[rows, :], gain1, xh1, sl1, rs1)
            gf_ref[rows, :] = (cot_ref[rows, :].astype(F32) * alive[n] + grad).astype(BF16)

        chunks(4, 128, grad_rows)
    store(gf_ref, gf_hbm, 1)

    for j in range(1, 8):
        start = pl.multiple_of((ci + j % 2) % 2 * 1024 + (y - j // 2 + YD) % YD * 256, 256)
        wait(fin.at[pl.ds(start, 256)], ag_sem.at[1, 1, j])
    fout[...] = fin[pl.ds(0, 1808), :].astype(F32)
    store(fout.at[pl.ds(0, 896)], gw1_hbm, 2)
    store(fout.at[pl.ds(896, 896)], gw2_hbm, 3)
    store(fout.at[pl.ds(1792, 1)], gg1_hbm, 4)
    store(fout.at[pl.ds(1793, 1)], gg2_hbm, 5)

    for pay in range(4):
        for o in (1, 2, 3, 5, 6, 7):
            for k in range(2):
                wait(part(pay, o, k), ring_send.at[pay, o, k])
        for group in range(4):
            wait(outb.at[(pay, *flying(group))], x_send.at[pay, group])
    wait(tbl.at[pl.ds(1, 7)], t_sem.at[0])
    wait(ay_out.at[pl.ds(1, 7)], ar_sem.at[0, 0])
    wait(ax_out.at[pl.ds(1, 3)], ar_sem.at[1, 0])
    wait(az.at[pl.ds(1, 7)], ar_sem.at[2, 0])
    for o in range(1, XD):
        wait(fin.at[pl.ds(mine_x, 64)], ag_sem.at[0, 0, o])
    for j in range(1, 8):
        wait(fin.at[pl.ds(mine, 256)], ag_sem.at[1, 0, j])
    for i, ref in enumerate((out_ref, gf_ref)):
        wait(ref, st_sem.at[i])
    for i in range(2):
        wait(fout.at[pl.ds(0, 896)], st_sem.at[2 + i])
        wait(fout.at[pl.ds(1792, 1)], st_sem.at[4 + i])


def hand_over(*refs):
    sems = refs[18]
    loads = [pltpu.make_async_copy(refs[i], refs[12 + i], sems.at[0, i]) for i in range(6)]
    stores = [pltpu.make_async_copy(refs[12 + i], refs[6 + i], sems.at[1, i]) for i in range(6)]
    for copy in loads:
        copy.start()
    for copy, store in zip(loads, stores):
        copy.wait()
        store.start()
    for store in stores:
        store.wait()


def shards(
    features, gain_one, weight_one, gain_two, weight_two, live, send_index, recv_index, cotangent
):
    scale = 1.0 / math.sqrt(
        features.shape[1] * features.shape[2] * lax.axis_size("shape") * lax.axis_size("space")
    )
    rows = 1024
    smem = pl.BlockSpec(memory_space=pltpu.SMEM)
    hbm = pl.BlockSpec(memory_space=pltpu.HBM)
    shapes = [
        jax.ShapeDtypeStruct((rows, 128), BF16),
        jax.ShapeDtypeStruct((rows, 128), BF16),
        jax.ShapeDtypeStruct((896, 128), F32),
        jax.ShapeDtypeStruct((896, 128), F32),
        jax.ShapeDtypeStruct((1, 128), F32),
        jax.ShapeDtypeStruct((1, 128), F32),
    ]
    results = pl.pallas_call(
        functools.partial(kernel, scale),
        out_shape=shapes,
        in_specs=[smem] * 3 + [hbm] * 6,
        out_specs=[hbm] * 6,
        scratch_shapes=[
            *[pltpu.VMEM((2, 6, 64, 128), BF16)] * 32,
            *[pltpu.VMEM((8, 8, 64, 128), BF16)] * 4,
            pltpu.VMEM((4, 8, 8, 64, 128), BF16),
            pltpu.VMEM((8, 8, 128), jnp.int32),
            pltpu.SMEM((8, 8, 128), jnp.int32),
            pltpu.VMEM((80, 128), jnp.int32),
            pltpu.SMEM((80, 128), jnp.int32),
            pltpu.VMEM((64, 64, 128), F32),
            pltpu.VMEM((64, 128), jnp.int32),
            pltpu.VMEM((1808, 128), F32),
            pltpu.VMEM((rows, 128), BF16),
            pltpu.VMEM((rows, 128), BF16),
            pltpu.VMEM((896, 128), BF16),
            pltpu.VMEM((896, 128), BF16),
            pltpu.VMEM((2, 1, 128), F32),
            pltpu.VMEM((rows, 128), BF16),
            pltpu.VMEM((rows, 128), BF16),
            pltpu.VMEM((1040, 128), F32),
            pltpu.VMEM((512, 128), F32),
            pltpu.VMEM((128, 128), F32),
            pltpu.VMEM((rows, 896), BF16),
            pltpu.VMEM((rows, 896), BF16),
            pltpu.VMEM((rows, 128), BF16),
            *[pltpu.VMEM((rows, 128), F32)] * 8,
            pltpu.VMEM((12, 64, 128), BF16),
            pltpu.VMEM((12, 64, 128), F32),
            pltpu.VMEM((12, 64, 128), F32),
            pltpu.VMEM((896, 128), BF16),
            pltpu.VMEM((896, 128), BF16),
            pltpu.VMEM((2048, 128), F32),
            pltpu.VMEM((2048, 128), BF16),
            pltpu.VMEM((8, 256, 128), BF16),
            pltpu.VMEM((8, 256, 128), BF16),
            pltpu.VMEM((4, 64, 128), BF16),
            pltpu.VMEM((4, 64, 128), BF16),
            pltpu.VMEM((8, 64, 128), BF16),
            pltpu.SemaphoreType.DMA((4, 8, 2)),
            pltpu.SemaphoreType.DMA((4, 8, 2)),
            pltpu.SemaphoreType.DMA((4, 4)),
            pltpu.SemaphoreType.DMA((4, 4)),
            pltpu.SemaphoreType.DMA((2,)),
            pltpu.SemaphoreType.DMA((3, 2)),
            pltpu.SemaphoreType.DMA((2, 2, 8)),
            pltpu.SemaphoreType.DMA((8,)),
            pltpu.SemaphoreType.DMA((6,)),
        ],
        compiler_params=pltpu.CompilerParams(
            collective_id=0, has_side_effects=True, vmem_limit_bytes=56 * 1024 * 1024
        ),
    )(
        send_index.reshape(64),
        recv_index.reshape(2, 6),
        live.reshape(2),
        features.reshape(rows, 128),
        gain_one.reshape(1, 128),
        weight_one.reshape(896, 128),
        gain_two.reshape(1, 128),
        weight_two.reshape(896, 128),
        cotangent.reshape(rows, 128),
    )
    out, grad, w1, w2, g1, g2 = pl.pallas_call(
        hand_over,
        out_shape=shapes,
        in_specs=[hbm] * 6,
        out_specs=[hbm] * 6,
        scratch_shapes=[
            *[pltpu.VMEM(s.shape, s.dtype) for s in shapes],
            pltpu.SemaphoreType.DMA((2, 6)),
        ],
    )(*results)
    return (
        out.reshape(features.shape),
        grad.reshape(features.shape),
        w1.reshape(7, 128, 128),
        w2.reshape(7, 128, 128),
        g1.reshape(128),
        g2.reshape(128),
    )


def solution(mesh):
    bricks = P("shape", "space", None, None)
    in_specs = (
        bricks,
        P(),
        P(),
        P(),
        P(),
        P("shape", "space"),
        bricks,
        P("shape", "space", None),
        bricks,
    )
    out_specs = (bricks, bricks, P(), P(), P(), P())
    return jax.shard_map(shards, mesh=mesh, in_specs=in_specs, out_specs=out_specs, check_vma=False)
```

```python
import functools
import math

import jax
import jax.numpy as jnp
from jax import lax
from jax.experimental import pallas as pl
from jax.experimental.pallas import tpu as pltpu
from jax.sharding import PartitionSpec as P

MESH = pl.DeviceIdType.MESH
F32 = jnp.float32
BF16 = jnp.bfloat16
EPS = 1e-05
SWAP = (0, 2, 1, 4, 3, 6, 5)
XD, ZD, YD = 4, 8, 4
LO = 8
UNH = 4
UNC = 4
UNP = 4
POS = (0, 1, 3, 5, 7, 6, 4, 2)
GROUPS = ((0, 3), (3, 2), (5, 2), (7, 1))


def norm(v):
    c = v - jnp.mean(v, axis=-1, keepdims=True)
    r = lax.rsqrt(jnp.mean(c * c, axis=-1, keepdims=True) + EPS)
    return c * r, r


def silu_parts(t):
    s = 0.5 * jnp.tanh(0.5 * t) + 0.5
    return t * s, s * (1.0 + t * (1.0 - s))


def rounded(v):
    return v.astype(BF16).astype(F32)


def dot(a, b):
    return jnp.dot(a, b, preferred_element_type=F32)


def dot_t(a, b):
    return lax.dot_general(a, b, (((0,), (0,)), ((), ())), preferred_element_type=F32)


def kernel(
    scale,
    send_s,
    recv_s,
    live_s,
    x_hbm,
    g1_hbm,
    w1_hbm,
    g2_hbm,
    w2_hbm,
    cot_hbm,
    out_hbm,
    gf_hbm,
    gw1_hbm,
    gw2_hbm,
    gg1_hbm,
    gg2_hbm,
    *scratch,
):
    gath = [scratch[i * 8 : i * 8 + 8] for i in range(4)]
    inb = scratch[32:36]
    (
        outb,
        tbl,
        tbl_s,
        ordv,
        ord_s,
        seg,
        col,
        fout,
        x_ref,
        cot_ref,
        w1_ref,
        w2_ref,
        gains,
        out_ref,
        gf_ref,
        a32,
        s32,
        e32,
        u7,
        v7,
        act2,
        acc,
        acc2,
        xh1,
        sl1,
        rs1,
        xh2,
        sl2,
        rs2,
        hal,
        hald,
        ret,
        wt1,
        wt2,
        wg,
        fin,
        ac_out,
        ac_in,
        ay_out,
        ay_in,
        ax_out,
        ax_in,
        az,
        ring_send,
        ring_recv,
        x_send,
        x_recv,
        t_sem,
        ar_sem,
        ag_sem,
        ld_sem,
        st_sem,
    ) = scratch[36:]
    y = lax.axis_index("shape")
    sp = lax.axis_index("space")
    xi = sp // 16
    zi = (sp // 2) % ZD
    ci = sp % 2

    def dev(yy, xx, zz, cc):
        return (yy, (xx * ZD + zz) * 2 + cc)

    def z_dev(o):
        return dev(y, xi, (zi + o) % ZD, ci)

    def row_dev(l, step=0):
        return dev(y, (xi + l // 2) % XD, (zi + step + ZD) % ZD, (ci + l % 2) % 2)

    def row_source(l, step):
        return dev(y, (xi - l // 2 + XD) % XD, (zi + step + ZD) % ZD, (ci + l % 2) % 2)

    def x_dev(o):
        return dev(y, (xi + o) % XD, zi, ci)

    def y_dev(o):
        return dev((y + o) % YD, xi, zi, ci)

    barrier = pltpu.get_barrier_semaphore()

    def greet(target):
        pl.semaphore_signal(barrier, inc=1, device_id=target, device_id_type=MESH)

    for o in range(1, ZD):
        greet(z_dev(o))
    for l in range(1, 8):
        greet(row_dev(l))
    for o in range(1, YD):
        greet(y_dev(o))
    for l in range(1, 4):
        greet(row_source(l, -1))
    for l in range(4, 8):
        greet(row_source(l, 1))

    def load(src, dst, i):
        pltpu.make_async_copy(src, dst, ld_sem.at[i]).start()

    load(x_hbm, x_ref, 0)
    load(cot_hbm, cot_ref, 1)
    load(w1_hbm, w1_ref, 2)
    load(w2_hbm, w2_ref, 3)
    load(g1_hbm, gains.at[0], 4)
    load(g2_hbm, gains.at[1], 5)

    def push(src, dst, ssem, rsem, target):
        pltpu.make_async_remote_copy(
            src_ref=src,
            dst_ref=dst,
            send_sem=ssem,
            recv_sem=rsem,
            device_id=target,
            device_id_type=MESH,
        ).start()

    def wait(ref, sem):
        pltpu.make_async_copy(ref, ref, sem).wait()

    def part(pay, slot, k):
        if k == 0:
            return gath[pay][slot].at[:, pl.ds(0, 2)]
        return gath[pay][slot].at[:, pl.ds(2, 4), pl.ds(0, 48)]

    def ring(pay, src, dst, k, step):
        push(
            part(pay, src, k),
            part(pay, dst, k),
            ring_send.at[pay, dst, k],
            ring_recv.at[pay, dst, k],
            z_dev(step),
        )

    def forward(pay, h):
        for k in range(2):
            for src, dst, step in ((h, h + 1, 1), ((ZD - h) % ZD, ZD - 1 - h, ZD - 1)):
                if h > 0:
                    wait(part(pay, src, k), ring_recv.at[pay, src, k])
                if h < 3:
                    ring(pay, src, dst, k, step)

    def fill(pay, slot):
        g = gath[pay][slot]
        for n in range(2):
            e32[...] = g[n, 0:2].reshape(128, 128).astype(F32)
            g[n, 2, 48:64] = jnp.concatenate([e32[0:8], e32[64:72]], axis=0).astype(BF16)
            g[n, 3, 48:64] = jnp.concatenate([e32[56:64], e32[120:128]], axis=0).astype(BF16)
            g[n, 4, 48:64] = e32[pl.ds(0, 16, stride=8), :].astype(BF16)
            g[n, 5, 48:64] = e32[pl.ds(7, 16, stride=8), :].astype(BF16)

    def pick(pay, slot, o, l):
        code = jnp.maximum(tbl_s[slot, o, l + 8 * (pay % 2)], 0)
        slab = gath[pay][slot][code // 8, code % 8]
        if l == 0 and o == slot:
            inb[pay][0, POS[o]] = slab
        else:
            outb[pay, l, POS[o]] = slab

    def deliver(pay, group, l, step):
        first, count = GROUPS[group]
        push(
            outb.at[pay, l, pl.ds(first, count)],
            inb[pay].at[l, pl.ds(first, count)],
            x_send.at[pay, group],
            x_recv.at[pay, group],
            row_dev(l, step),
        )

    def select(pay, h):
        if h == 3:
            for l in range(4):
                pick(pay, 3, 4, l)
                deliver(pay, 3, l, 1)
            for l in range(4, 8):
                pick(pay, 5, 4, l)
                deliver(pay, 3, l, -1)
        for l in (4, 5, 2, 3, 6, 7, 1, 0):
            for o in ((0, 1, 7), (2, 6), (3, 5))[h - 1]:
                pick(pay, o, o, l)
            if l > 0:
                deliver(pay, h - 1, l, 0)

    def flying(group):
        first, count = GROUPS[group]
        return (pl.ds(0, 8) if group == 3 else pl.ds(1, 7)), pl.ds(first, count)

    def arrived(pay):
        for group in range(4):
            wait(inb[pay].at[flying(group)], x_recv.at[pay, group])

    def hop(pay, h):
        forward(pay, h)
        if h > 0:
            fill(pay, h)
            fill(pay, ZD - h)
            select(pay, h)

    def returns(pay):
        arrived(pay)

        def one(k, carry):
            total, before = carry
            v = ord_s[k, 0]
            code, at = v // 64, v % 64
            total = total * (code == before).astype(F32) + inb[pay][at // 8, at % 8].astype(F32)
            seg[k] = total
            return total, code

        lax.fori_loop(0, 64, one, (jnp.zeros((64, 128), F32), jnp.int32(-1)), unroll=8)

        def pickup(q, carry):
            start, end = ord_s[64 + q, 0], ord_s[65 + q, 0]
            ret[q] = seg[jnp.maximum(end - 1, 0)] * (end > start).astype(F32)
            return carry

        lax.fori_loop(0, 12, pickup, 0, unroll=4)

    def position(r):
        o = (zi - (r // 2) % ZD + ZD) % ZD
        l = ((xi - r // 16 + XD) % XD) * 2 + (ci + r % 2) % 2
        near = jnp.where(o < 4, jnp.maximum(2 * o - 1, 0), jnp.where(o > 4, 16 - 2 * o, 7))
        return l * 8 + near

    def take_halo(pay, q):
        r = recv_s[q // 6, q % 6]
        at = position(jnp.maximum(r, 0))
        return inb[pay][at // 8, at % 8].astype(F32) * (r >= 0).astype(F32)

    def chunks(n, size, body):
        def step(i, carry):
            body(pl.multiple_of(i * size, size))
            return carry

        lax.fori_loop(0, n, step, 0, unroll=UNC if size == 128 else UNP)

    def ordered(v):
        v = v.reshape(8, 8, 128)
        return jnp.concatenate([v[1:7], v[0:1], v[7:8]], axis=0).reshape(64, 128)

    def natural(v):
        v = v.reshape(8, 8, 128)
        return jnp.concatenate([v[6:7], v[0:6], v[7:8]], axis=0).reshape(64, 128)

    def faces(pay):
        g = gath[pay][0]
        for n in range(2):
            base = LO + n * 512
            cube = a32[pl.ds(base, 512), :].reshape(8, 8, 8, 128)
            g[n, 0] = a32[pl.ds(base, 64), :].astype(BF16)
            g[n, 1] = a32[pl.ds(base + 448, 64), :].astype(BF16)
            g[n, 2] = ordered(cube[:, 0]).astype(BF16)
            g[n, 3] = ordered(cube[:, 7]).astype(BF16)
            g[n, 4] = ordered(a32[pl.ds(base, 64, stride=8), :]).astype(BF16)
            g[n, 5] = ordered(a32[pl.ds(base + 7, 64, stride=8), :]).astype(BF16)

    def columns(dst):
        zero = jnp.zeros((64, 128), F32)
        plate = jnp.zeros((8, 1, 8, 128), F32)
        for n in range(2):
            base = LO + n * 512
            rows = pl.ds(n * 512, 512)
            body = a32[pl.ds(base, 512), :]
            half = body.astype(BF16)
            dst[rows, 0:128] = half
            dst[pl.ds(n * 512, 64), 128:256] = zero.astype(BF16)
            dst[pl.ds(n * 512 + 64, 448), 128:256] = half[:448]
            dst[pl.ds(n * 512, 448), 256:384] = half[64:]
            dst[pl.ds(n * 512 + 448, 64), 256:384] = zero.astype(BF16)
            cube = body.reshape(8, 8, 8, 128)
            low = jnp.concatenate([plate, cube[:, :7]], axis=1)
            dst[rows, 384:512] = low.reshape(512, 128).astype(BF16)
            high = jnp.concatenate([cube[:, 1:], plate], axis=1)
            dst[rows, 512:640] = high.reshape(512, 128).astype(BF16)
            s32[...] = a32[pl.ds(base - 1, 512), :]
            s32[pl.ds(0, 64, stride=8), :] = zero
            dst[rows, 640:768] = s32[...].astype(BF16)
            s32[...] = a32[pl.ds(base + 1, 512), :]
            s32[pl.ds(7, 64, stride=8), :] = zero
            dst[rows, 768:896] = s32[...].astype(BF16)

    def add_face(target, n, f, term):
        base = n * 512
        if f == 0:
            target[pl.ds(base, 64), :] += term
        elif f == 1:
            target[pl.ds(base + 448, 64), :] += term
        elif f < 4:
            term = natural(term)
            for i in range(8):
                target[pl.ds(base + i * 64 + (f - 2) * 56, 8), :] += term[i * 8 : i * 8 + 8]
        else:
            rows = pl.ds(base + (f - 4) * 7, 64, stride=8)
            target[rows, :] = target[rows, :] + natural(term)

    def add_faces(target, slab, w):
        for f in range(6):
            both = jnp.concatenate([slab(f), slab(6 + f)], axis=0)
            term = dot(both, w[pl.ds((f + 1) * 128, 128), :])
            add_face(target, 0, f, term[:64])
            add_face(target, 1, f, term[64:])

    def product(target, cols, w):
        def rows_of(r):
            rows = pl.ds(r, 256)
            target[rows, :] = dot(cols[rows, :], w[...])

        chunks(4, 256, rows_of)

    def back_rows(r, up, gain, xh, sl, rs):
        rows = pl.ds(r, 128)
        xhat = xh[rows, :]
        dt = up * sl[rows, :]
        d = dt * gain
        mean_d = jnp.mean(d, axis=-1, keepdims=True)
        mean_dx = jnp.mean(d * xhat, axis=-1, keepdims=True)
        return rs[rows, :] * (d - mean_d - xhat * mean_dx), dt * xhat

    def pre_rows(v, r, gain, xh, sl, rs):
        rows = pl.ds(r, 128)
        xhat, inv = norm(v)
        a, slope = silu_parts(xhat * gain)
        xh[rows, :] = xhat
        sl[rows, :] = slope
        rs[rows, :] = jnp.broadcast_to(inv, (128, 128))
        return a

    alive = [live_s[n].astype(F32) for n in range(2)]

    step_id = lax.broadcasted_iota(jnp.int32, (8, 128), 0)
    lane_id = lax.broadcasted_iota(jnp.int32, (8, 128), 1)
    in_x = lane_id % 8
    target_id = (
        ((xi + in_x // 2) % XD) * (2 * ZD) + ((zi + step_id) % ZD) * 2 + (ci + in_x % 2) % 2
    )
    codes = jnp.full((8, 128), -1, jnp.int32)
    for e in range(64):
        codes = jnp.where(target_id == e, send_s[e], codes)
    back = jnp.full((8, 128), -1, jnp.int32)
    for q in range(12):
        back = jnp.where(target_id == recv_s[q // 6, q % 6], q, back)
    chosen = jnp.where(lane_id < 8, codes, back)
    tbl[0] = chosen + 2 * (chosen >= 6).astype(jnp.int32)

    wait(x_ref, ld_sem.at[0])
    a32[pl.ds(LO, 1024), :] = x_ref[...].astype(F32)
    faces(0)
    pl.semaphore_wait(barrier, 24)
    for o in range(1, ZD):
        push(tbl.at[0], tbl.at[o], t_sem.at[0], t_sem.at[1], z_dev(o))
    forward(0, 0)

    lane = lax.broadcasted_iota(jnp.int32, (64, 128), 1)
    line = lax.broadcasted_iota(jnp.int32, (64, 128), 0)
    across = jnp.full((8, 128), 99, jnp.int32)
    for e in range(64):
        across = jnp.where(lane_id == e, send_s[e], across)
        col[pl.ds(e, 1), :] = jnp.full((1, 128), send_s[e], jnp.int32)
    across = jnp.broadcast_to(across[0:1], (64, 128))
    down = col[...]
    ahead = (down < across) | ((down == across) & (line < lane))
    rank = jnp.sum(ahead.astype(jnp.int32), axis=0, keepdims=True)
    value = position(jnp.minimum(lane, 63)) + 64 * (jnp.minimum(across, 15) + 1)
    sorted_values = jnp.sum(
        jnp.where((rank == line) & (lane < 64), value, 0), axis=1, keepdims=True
    )
    ordv[pl.ds(0, 64), :] = jnp.broadcast_to(sorted_values, (64, 128))
    below = jnp.sum((across < line).astype(jnp.int32), axis=1, keepdims=True)
    ordv[pl.ds(64, 16), :] = jnp.broadcast_to(below, (64, 128))[:16]
    pltpu.make_async_copy(ordv, ord_s, ld_sem.at[7]).start()

    wait(cot_ref, ld_sem.at[1])
    for n in range(2):
        a32[pl.ds(LO + n * 512, 512), :] = cot_ref[pl.ds(n * 512, 512), :].astype(F32) * alive[n]
    faces(1)
    columns(v7)
    wait(tbl.at[pl.ds(1, 7)], t_sem.at[1])
    codes_in = pltpu.make_async_copy(tbl, tbl_s, ld_sem.at[6])
    codes_in.start()
    codes_in.wait()
    hop(0, 1)

    wait(gains.at[0], ld_sem.at[4])
    wait(gains.at[1], ld_sem.at[5])
    gain1 = gains[0]
    gain2 = gains[1]

    def act_one(r):
        a = pre_rows(x_ref[pl.ds(r, 128), :].astype(F32), r, gain1, xh1, sl1, rs1)
        a32[pl.ds(LO + r, 128), :] = rounded(a)

    chunks(8, 128, act_one)
    hop(0, 2)
    hop(1, 0)
    columns(u7)
    wait(w1_ref, ld_sem.at[2])
    wait(w2_ref, ld_sem.at[3])
    product(acc, u7, w1_ref)
    hop(0, 3)
    for t in range(7):
        src = pl.ds(SWAP[t] * 128, 128)
        wt1[pl.ds(t * 128, 128), :] = w1_ref[src, :].astype(F32).T.astype(BF16)
        wt2[pl.ds(t * 128, 128), :] = w2_ref[src, :].astype(F32).T.astype(BF16)
    product(acc2, v7, wt2)
    hop(1, 1)

    arrived(0)

    def halo_one(q, carry):
        xhat, _ = norm(take_halo(0, q))
        act, slope = silu_parts(xhat * gain1)
        hal[q] = act.astype(BF16)
        hald[q] = slope * xhat
        return carry

    lax.fori_loop(0, 12, halo_one, 0, unroll=UNH)
    add_faces(acc, lambda q: hal[q], w1_ref)

    def hidden_rows(r):
        rows = pl.ds(r, 128)
        a = pre_rows(rounded(acc[rows, :]), r, gain2, xh2, sl2, rs2).astype(BF16)
        act2[rows, :] = a
        a32[pl.ds(LO + r, 128), :] = a.astype(F32)

    chunks(8, 128, hidden_rows)
    faces(2)
    hop(1, 2)
    hop(2, 0)

    hop(1, 3)
    hop(2, 1)
    pltpu.make_async_copy(ordv, ord_s, ld_sem.at[7]).wait()
    returns(1)
    add_faces(acc2, lambda q: ret[q].astype(BF16), wt2)
    wg[pl.ds(1792, 256), :] = jnp.zeros((256, 128), F32)

    def grad_hidden_rows(r):
        grad, per = back_rows(r, acc2[pl.ds(r, 128), :], gain2, xh2, sl2, rs2)
        a32[pl.ds(LO + r, 128), :] = rounded(grad)
        wg[pl.ds(1793, 1), :] += jnp.sum(per, axis=0, keepdims=True)

    chunks(8, 128, grad_hidden_rows)
    faces(3)
    hop(3, 0)
    hop(2, 2)

    def slabs(pay, f):
        return gath[pay][0][:, f].reshape(128, 128)

    a2 = act2[...]
    for t in range(7):
        total = dot_t(a2, v7[:, t * 128 : t * 128 + 128])
        if t > 0:
            r2 = jnp.concatenate([ret[t - 1], ret[t + 5]], axis=0).astype(BF16)
            total = total + dot_t(slabs(2, t - 1), r2)
        wg[pl.ds(896 + SWAP[t] * 128, 128), :] = total
    gh = a32[pl.ds(LO, 1024), :].astype(BF16)
    for t in range(7):
        total = dot_t(u7[:, t * 128 : t * 128 + 128], gh)
        if t > 0:
            h2 = jnp.concatenate([hal[t - 1], hal[t + 5]], axis=0)
            total = total + dot_t(h2, slabs(3, t - 1))
        wg[pl.ds(t * 128, 128), :] = total

    columns(v7)
    product(acc2, v7, wt1)

    def gain_rows(r):
        rows = pl.ds(r, 128)
        per = acc2[rows, :] * sl1[rows, :] * xh1[rows, :]
        wg[pl.ds(1792, 1), :] += jnp.sum(per, axis=0, keepdims=True)

    chunks(8, 128, gain_rows)
    for f in range(6):
        both = dot(slabs(3, f), wt1[pl.ds(SWAP[f + 1] * 128, 128), :])
        slope = jnp.concatenate([hald[f], hald[6 + f]], axis=0)
        wg[pl.ds(1792, 1), :] += jnp.sum(rounded(both) * slope, axis=0, keepdims=True)

    half = pl.multiple_of(ci * 1024, 1024)
    other = pl.multiple_of((1 - ci) * 1024, 1024)
    mine = pl.multiple_of(half + y * 256, 256)
    ac_out[...] = wg[pl.ds(other, 1024), :].astype(BF16)
    push(ac_out, ac_in, ar_sem.at[3, 0], ar_sem.at[3, 1], row_dev(1))

    hop(3, 1)
    wait(ac_in, ar_sem.at[3, 1])
    wg[pl.ds(half, 1024), :] += ac_in[...].astype(F32)
    for o in range(1, YD):
        start = pl.multiple_of(half + (y + o) % YD * 256, 256)
        ay_out[o] = wg[pl.ds(start, 256), :].astype(BF16)
        push(ay_out.at[o], ay_in.at[o], ar_sem.at[0, 0], ar_sem.at[0, 1], y_dev(o))
    hop(2, 3)

    a32[pl.ds(LO, 1024), :] = act2[...].astype(F32)
    columns(u7)
    product(acc, u7, w2_ref)

    wait(ay_in.at[pl.ds(1, 3)], ar_sem.at[0, 1])
    partial = wg[pl.ds(mine, 256), :]
    for o in range(1, YD):
        partial = partial + ay_in[o].astype(F32)
    wg[pl.ds(mine, 256), :] = partial
    for o in range(1, XD):
        start = pl.multiple_of(mine + ((xi + o) % XD) * 64, 64)
        ax_out[o] = wg[pl.ds(start, 64), :].astype(BF16)
        push(ax_out.at[o], ax_in.at[o], ar_sem.at[1, 0], ar_sem.at[1, 1], x_dev(o))

    hop(3, 2)

    wait(ax_in.at[pl.ds(1, 3)], ar_sem.at[1, 1])
    mine_x = pl.multiple_of(mine + xi * 64, 64)
    partial = wg[pl.ds(mine_x, 64), :]
    for o in range(1, XD):
        partial = partial + ax_in[o].astype(F32)
    az[0] = partial.astype(BF16)
    for o in range(1, ZD):
        push(az.at[0], az.at[o], ar_sem.at[2, 0], ar_sem.at[2, 1], z_dev(o))

    arrived(2)
    add_faces(acc, lambda q: take_halo(2, q).astype(BF16), w2_ref)
    for n in range(2):
        rows = pl.ds(n * 512, 512)
        out_ref[rows, :] = ((x_ref[rows, :].astype(F32) + acc[rows, :]) * alive[n]).astype(BF16)

    def store(src, dst, i):
        pltpu.make_async_copy(src, dst, st_sem.at[i]).start()

    store(out_ref, out_hbm, 0)

    hop(3, 3)
    wait(az.at[pl.ds(1, 7)], ar_sem.at[2, 1])
    total = jnp.zeros((64, 128), F32)
    for k in range(ZD):
        total = total + az[(zi - k + ZD) % ZD].astype(F32)
    fin[pl.ds(mine_x, 64), :] = (total * scale).astype(BF16)
    piece = fin.at[pl.ds(mine_x, 64)]
    for o in range(1, XD):
        push(piece, piece, ag_sem.at[0, 0, o], ag_sem.at[0, 1, o], x_dev(o))

    def gather_y():
        for o in range(1, XD):
            start = pl.multiple_of(mine + ((xi - o + XD) % XD) * 64, 64)
            wait(fin.at[pl.ds(start, 64)], ag_sem.at[0, 1, o])
        piece = fin.at[pl.ds(mine, 256)]
        for o in range(1, YD):
            push(piece, piece, ag_sem.at[1, 0, o], ag_sem.at[1, 1, o], y_dev(o))

    returns(3)
    gather_y()
    add_faces(acc2, lambda q: ret[q].astype(BF16), wt1)
    for n in range(2):

        def grad_rows(i, n=n):
            r = pl.multiple_of(n * 512 + i, 128)
            rows = pl.ds(r, 128)
            grad, _ = back_rows(r, acc2[rows, :], gain1, xh1, sl1, rs1)
            gf_ref[rows, :] = (cot_ref[rows, :].astype(F32) * alive[n] + grad).astype(BF16)

        chunks(4, 128, grad_rows)
    store(gf_ref, gf_hbm, 1)

    for o in range(1, YD):
        start = pl.multiple_of(half + (y - o + YD) % YD * 256, 256)
        wait(fin.at[pl.ds(start, 256)], ag_sem.at[1, 1, o])
    piece = fin.at[pl.ds(half, 1024)]
    push(piece, piece, ag_sem.at[2, 0, 0], ag_sem.at[2, 1, 0], row_dev(1))
    wait(fin.at[pl.ds(other, 1024)], ag_sem.at[2, 1, 0])
    fout[...] = fin[pl.ds(0, 1808), :].astype(F32)
    store(fout.at[pl.ds(0, 896)], gw1_hbm, 2)
    store(fout.at[pl.ds(896, 896)], gw2_hbm, 3)
    store(fout.at[pl.ds(1792, 1)], gg1_hbm, 4)
    store(fout.at[pl.ds(1793, 1)], gg2_hbm, 5)

    for pay in range(4):
        for o in (1, 2, 3, 5, 6, 7):
            for k in range(2):
                wait(part(pay, o, k), ring_send.at[pay, o, k])
        for group in range(4):
            wait(outb.at[(pay, *flying(group))], x_send.at[pay, group])
    wait(tbl.at[pl.ds(1, 7)], t_sem.at[0])
    wait(ac_out, ar_sem.at[3, 0])
    wait(ay_out.at[pl.ds(1, 3)], ar_sem.at[0, 0])
    wait(ax_out.at[pl.ds(1, 3)], ar_sem.at[1, 0])
    wait(az.at[pl.ds(1, 7)], ar_sem.at[2, 0])
    for o in range(1, XD):
        wait(fin.at[pl.ds(mine_x, 64)], ag_sem.at[0, 0, o])
    for o in range(1, YD):
        wait(fin.at[pl.ds(mine, 256)], ag_sem.at[1, 0, o])
    wait(fin.at[pl.ds(half, 1024)], ag_sem.at[2, 0, 0])
    for i, ref in enumerate((out_ref, gf_ref)):
        wait(ref, st_sem.at[i])
    for i in range(2):
        wait(fout.at[pl.ds(0, 896)], st_sem.at[2 + i])
        wait(fout.at[pl.ds(1792, 1)], st_sem.at[4 + i])


def hand_over(*refs):
    sems = refs[18]
    loads = [pltpu.make_async_copy(refs[i], refs[12 + i], sems.at[0, i]) for i in range(6)]
    stores = [pltpu.make_async_copy(refs[12 + i], refs[6 + i], sems.at[1, i]) for i in range(6)]
    for copy in loads:
        copy.start()
    for copy, store in zip(loads, stores):
        copy.wait()
        store.start()
    for store in stores:
        store.wait()


def shards(
    features, gain_one, weight_one, gain_two, weight_two, live, send_index, recv_index, cotangent
):
    scale = 1.0 / math.sqrt(
        features.shape[1] * features.shape[2] * lax.axis_size("shape") * lax.axis_size("space")
    )
    rows = 1024
    smem = pl.BlockSpec(memory_space=pltpu.SMEM)
    hbm = pl.BlockSpec(memory_space=pltpu.HBM)
    shapes = [
        jax.ShapeDtypeStruct((rows, 128), BF16),
        jax.ShapeDtypeStruct((rows, 128), BF16),
        jax.ShapeDtypeStruct((896, 128), F32),
        jax.ShapeDtypeStruct((896, 128), F32),
        jax.ShapeDtypeStruct((1, 128), F32),
        jax.ShapeDtypeStruct((1, 128), F32),
    ]
    results = pl.pallas_call(
        functools.partial(kernel, scale),
        out_shape=shapes,
        in_specs=[smem] * 3 + [hbm] * 6,
        out_specs=[hbm] * 6,
        scratch_shapes=[
            *[pltpu.VMEM((2, 6, 64, 128), BF16)] * 32,
            *[pltpu.VMEM((8, 8, 64, 128), BF16)] * 4,
            pltpu.VMEM((4, 8, 8, 64, 128), BF16),
            pltpu.VMEM((8, 8, 128), jnp.int32),
            pltpu.SMEM((8, 8, 128), jnp.int32),
            pltpu.VMEM((80, 128), jnp.int32),
            pltpu.SMEM((80, 128), jnp.int32),
            pltpu.VMEM((64, 64, 128), F32),
            pltpu.VMEM((64, 128), jnp.int32),
            pltpu.VMEM((1808, 128), F32),
            pltpu.VMEM((rows, 128), BF16),
            pltpu.VMEM((rows, 128), BF16),
            pltpu.VMEM((896, 128), BF16),
            pltpu.VMEM((896, 128), BF16),
            pltpu.VMEM((2, 1, 128), F32),
            pltpu.VMEM((rows, 128), BF16),
            pltpu.VMEM((rows, 128), BF16),
            pltpu.VMEM((1040, 128), F32),
            pltpu.VMEM((512, 128), F32),
            pltpu.VMEM((128, 128), F32),
            pltpu.VMEM((rows, 896), BF16),
            pltpu.VMEM((rows, 896), BF16),
            pltpu.VMEM((rows, 128), BF16),
            *[pltpu.VMEM((rows, 128), F32)] * 8,
            pltpu.VMEM((12, 64, 128), BF16),
            pltpu.VMEM((12, 64, 128), F32),
            pltpu.VMEM((12, 64, 128), F32),
            pltpu.VMEM((896, 128), BF16),
            pltpu.VMEM((896, 128), BF16),
            pltpu.VMEM((2048, 128), F32),
            pltpu.VMEM((2048, 128), BF16),
            pltpu.VMEM((1024, 128), BF16),
            pltpu.VMEM((1024, 128), BF16),
            pltpu.VMEM((4, 256, 128), BF16),
            pltpu.VMEM((4, 256, 128), BF16),
            pltpu.VMEM((4, 64, 128), BF16),
            pltpu.VMEM((4, 64, 128), BF16),
            pltpu.VMEM((8, 64, 128), BF16),
            pltpu.SemaphoreType.DMA((4, 8, 2)),
            pltpu.SemaphoreType.DMA((4, 8, 2)),
            pltpu.SemaphoreType.DMA((4, 4)),
            pltpu.SemaphoreType.DMA((4, 4)),
            pltpu.SemaphoreType.DMA((2,)),
            pltpu.SemaphoreType.DMA((4, 2)),
            pltpu.SemaphoreType.DMA((3, 2, 4)),
            pltpu.SemaphoreType.DMA((8,)),
            pltpu.SemaphoreType.DMA((6,)),
        ],
        compiler_params=pltpu.CompilerParams(
            collective_id=0, has_side_effects=True, vmem_limit_bytes=56 * 1024 * 1024
        ),
    )(
        send_index.reshape(64),
        recv_index.reshape(2, 6),
        live.reshape(2),
        features.reshape(rows, 128),
        gain_one.reshape(1, 128),
        weight_one.reshape(896, 128),
        gain_two.reshape(1, 128),
        weight_two.reshape(896, 128),
        cotangent.reshape(rows, 128),
    )
    out, grad, w1, w2, g1, g2 = pl.pallas_call(
        hand_over,
        out_shape=shapes,
        in_specs=[hbm] * 6,
        out_specs=[hbm] * 6,
        scratch_shapes=[
            *[pltpu.VMEM(s.shape, s.dtype) for s in shapes],
            pltpu.SemaphoreType.DMA((2, 6)),
        ],
    )(*results)
    return (
        out.reshape(features.shape),
        grad.reshape(features.shape),
        w1.reshape(7, 128, 128),
        w2.reshape(7, 128, 128),
        g1.reshape(128),
        g2.reshape(128),
    )


def solution(mesh):
    bricks = P("shape", "space", None, None)
    in_specs = (
        bricks,
        P(),
        P(),
        P(),
        P(),
        P("shape", "space"),
        bricks,
        P("shape", "space", None),
        bricks,
    )
    out_specs = (bricks, bricks, P(), P(), P(), P())
    return jax.shard_map(shards, mesh=mesh, in_specs=in_specs, out_specs=out_specs, check_vma=False)
```

```python
import functools
import math

import jax
import jax.numpy as jnp
from jax import lax
from jax.experimental import pallas as pl
from jax.experimental.pallas import tpu as pltpu
from jax.sharding import PartitionSpec as P

MESH = pl.DeviceIdType.MESH
F32 = jnp.float32
BF16 = jnp.bfloat16
EPS = 1e-05
SWAP = (0, 2, 1, 4, 3, 6, 5)
XD, ZD, YD = 4, 8, 4
LO = 8
UNH = 4
UNC = 4
UNP = 4
POS = (0, 1, 3, 5, 7, 6, 4, 2)
GROUPS = ((0, 3), (3, 2), (5, 2), (7, 1))


def norm(v):
    c = v - jnp.mean(v, axis=-1, keepdims=True)
    r = lax.rsqrt(jnp.mean(c * c, axis=-1, keepdims=True) + EPS)
    return c * r, r


def silu_parts(t):
    s = 0.5 * jnp.tanh(0.5 * t) + 0.5
    return t * s, s * (1.0 + t * (1.0 - s))


def rounded(v):
    return v.astype(BF16).astype(F32)


def dot(a, b):
    return jnp.dot(a, b, preferred_element_type=F32)


def dot_t(a, b):
    return lax.dot_general(a, b, (((0,), (0,)), ((), ())), preferred_element_type=F32)


def kernel(
    scale,
    send_s,
    recv_s,
    live_s,
    x_hbm,
    g1_hbm,
    w1_hbm,
    g2_hbm,
    w2_hbm,
    cot_hbm,
    out_ref,
    gf_ref,
    gw1_ref,
    gw2_ref,
    gg1_ref,
    gg2_ref,
    *scratch,
):
    gath = [scratch[i * 8 : i * 8 + 8] for i in range(4)]
    inb = scratch[32:36]
    (
        outb,
        tbl,
        tbl_s,
        ordv,
        ord_s,
        seg,
        col,
        x_ref,
        cot_ref,
        w1_ref,
        w2_ref,
        gains,
        a32,
        s32,
        e32,
        u7,
        v7,
        act2,
        acc,
        acc2,
        xh1,
        sl1,
        rs1,
        xh2,
        sl2,
        rs2,
        hal,
        hald,
        ret,
        wt1,
        wt2,
        wg,
        fin,
        ac_out,
        ac_in,
        ay_out,
        ay_in,
        ax_out,
        ax_in,
        az,
        ring_send,
        ring_recv,
        x_send,
        x_recv,
        t_sem,
        ar_sem,
        ag_sem,
        ld_sem,
    ) = scratch[36:]
    y = lax.axis_index("shape")
    sp = lax.axis_index("space")
    xi = sp // 16
    zi = (sp // 2) % ZD
    ci = sp % 2

    def dev(yy, xx, zz, cc):
        return (yy, (xx * ZD + zz) * 2 + cc)

    def z_dev(o):
        return dev(y, xi, (zi + o) % ZD, ci)

    def row_dev(l, step=0):
        return dev(y, (xi + l // 2) % XD, (zi + step + ZD) % ZD, (ci + l % 2) % 2)

    def row_source(l, step):
        return dev(y, (xi - l // 2 + XD) % XD, (zi + step + ZD) % ZD, (ci + l % 2) % 2)

    def x_dev(o):
        return dev(y, (xi + o) % XD, zi, ci)

    def y_dev(o):
        return dev((y + o) % YD, xi, zi, ci)

    barrier = pltpu.get_barrier_semaphore()

    def greet(target):
        pl.semaphore_signal(barrier, inc=1, device_id=target, device_id_type=MESH)

    for o in range(1, ZD):
        greet(z_dev(o))
    for l in range(1, 8):
        greet(row_dev(l))
    for o in range(1, YD):
        greet(y_dev(o))
    for l in range(1, 4):
        greet(row_source(l, -1))
    for l in range(4, 8):
        greet(row_source(l, 1))

    def load(src, dst, i):
        pltpu.make_async_copy(src, dst, ld_sem.at[i]).start()

    load(x_hbm, x_ref, 0)
    load(cot_hbm, cot_ref, 1)
    load(w1_hbm, w1_ref, 2)
    load(w2_hbm, w2_ref, 3)
    load(g1_hbm, gains.at[0], 4)
    load(g2_hbm, gains.at[1], 5)

    def push(src, dst, ssem, rsem, target):
        pltpu.make_async_remote_copy(
            src_ref=src,
            dst_ref=dst,
            send_sem=ssem,
            recv_sem=rsem,
            device_id=target,
            device_id_type=MESH,
        ).start()

    def wait(ref, sem):
        pltpu.make_async_copy(ref, ref, sem).wait()

    def part(pay, slot, k):
        if k == 0:
            return gath[pay][slot].at[:, pl.ds(0, 2)]
        return gath[pay][slot].at[:, pl.ds(2, 4), pl.ds(0, 48)]

    def ring(pay, src, dst, k, step):
        push(
            part(pay, src, k),
            part(pay, dst, k),
            ring_send.at[pay, dst, k],
            ring_recv.at[pay, dst, k],
            z_dev(step),
        )

    def forward(pay, h):
        for k in range(2):
            for src, dst, step in ((h, h + 1, 1), ((ZD - h) % ZD, ZD - 1 - h, ZD - 1)):
                if h > 0:
                    wait(part(pay, src, k), ring_recv.at[pay, src, k])
                if h < 3:
                    ring(pay, src, dst, k, step)

    def fill(pay, slot):
        g = gath[pay][slot]
        for n in range(2):
            e32[...] = g[n, 0:2].reshape(128, 128).astype(F32)
            g[n, 2, 48:64] = jnp.concatenate([e32[0:8], e32[64:72]], axis=0).astype(BF16)
            g[n, 3, 48:64] = jnp.concatenate([e32[56:64], e32[120:128]], axis=0).astype(BF16)
            g[n, 4, 48:64] = e32[pl.ds(0, 16, stride=8), :].astype(BF16)
            g[n, 5, 48:64] = e32[pl.ds(7, 16, stride=8), :].astype(BF16)

    def pick(pay, slot, o, l):
        code = jnp.maximum(tbl_s[slot, o, l + 8 * (pay % 2)], 0)
        slab = gath[pay][slot][code // 8, code % 8]
        if l == 0 and o == slot:
            inb[pay][0, POS[o]] = slab
        else:
            outb[pay, l, POS[o]] = slab

    def deliver(pay, group, l, step):
        first, count = GROUPS[group]
        push(
            outb.at[pay, l, pl.ds(first, count)],
            inb[pay].at[l, pl.ds(first, count)],
            x_send.at[pay, group],
            x_recv.at[pay, group],
            row_dev(l, step),
        )

    def select(pay, h):
        if h == 3:
            for l in range(4):
                pick(pay, 3, 4, l)
                deliver(pay, 3, l, 1)
            for l in range(4, 8):
                pick(pay, 5, 4, l)
                deliver(pay, 3, l, -1)
        for l in (4, 5, 2, 3, 6, 7, 1, 0):
            for o in ((0, 1, 7), (2, 6), (3, 5))[h - 1]:
                pick(pay, o, o, l)
            if l > 0:
                deliver(pay, h - 1, l, 0)

    def flying(group):
        first, count = GROUPS[group]
        return (pl.ds(0, 8) if group == 3 else pl.ds(1, 7)), pl.ds(first, count)

    def arrived(pay):
        for group in range(4):
            wait(inb[pay].at[flying(group)], x_recv.at[pay, group])

    def hop(pay, h):
        forward(pay, h)
        if h > 0:
            fill(pay, h)
            fill(pay, ZD - h)
            select(pay, h)

    def returns(pay):
        arrived(pay)

        def one(k, carry):
            total, before = carry
            v = ord_s[k, 0]
            code, at = v // 64, v % 64
            total = total * (code == before).astype(F32) + inb[pay][at // 8, at % 8].astype(F32)
            seg[k] = total
            return total, code

        lax.fori_loop(0, 64, one, (jnp.zeros((64, 128), F32), jnp.int32(-1)), unroll=8)

        def pickup(q, carry):
            start, end = ord_s[64 + q, 0], ord_s[65 + q, 0]
            ret[q] = seg[jnp.maximum(end - 1, 0)] * (end > start).astype(F32)
            return carry

        lax.fori_loop(0, 12, pickup, 0, unroll=4)

    def position(r):
        o = (zi - (r // 2) % ZD + ZD) % ZD
        l = ((xi - r // 16 + XD) % XD) * 2 + (ci + r % 2) % 2
        near = jnp.where(o < 4, jnp.maximum(2 * o - 1, 0), jnp.where(o > 4, 16 - 2 * o, 7))
        return l * 8 + near

    def take_halo(pay, q):
        r = recv_s[q // 6, q % 6]
        at = position(jnp.maximum(r, 0))
        return inb[pay][at // 8, at % 8].astype(F32) * (r >= 0).astype(F32)

    def chunks(n, size, body):
        def step(i, carry):
            body(pl.multiple_of(i * size, size))
            return carry

        lax.fori_loop(0, n, step, 0, unroll=UNC if size == 128 else UNP)

    def ordered(v):
        v = v.reshape(8, 8, 128)
        return jnp.concatenate([v[1:7], v[0:1], v[7:8]], axis=0).reshape(64, 128)

    def natural(v):
        v = v.reshape(8, 8, 128)
        return jnp.concatenate([v[6:7], v[0:6], v[7:8]], axis=0).reshape(64, 128)

    def faces(pay):
        g = gath[pay][0]
        for n in range(2):
            base = LO + n * 512
            cube = a32[pl.ds(base, 512), :].reshape(8, 8, 8, 128)
            g[n, 0] = a32[pl.ds(base, 64), :].astype(BF16)
            g[n, 1] = a32[pl.ds(base + 448, 64), :].astype(BF16)
            g[n, 2] = ordered(cube[:, 0]).astype(BF16)
            g[n, 3] = ordered(cube[:, 7]).astype(BF16)
            g[n, 4] = ordered(a32[pl.ds(base, 64, stride=8), :]).astype(BF16)
            g[n, 5] = ordered(a32[pl.ds(base + 7, 64, stride=8), :]).astype(BF16)

    def columns(dst):
        zero = jnp.zeros((64, 128), F32)
        plate = jnp.zeros((8, 1, 8, 128), F32)
        for n in range(2):
            base = LO + n * 512
            rows = pl.ds(n * 512, 512)
            body = a32[pl.ds(base, 512), :]
            half = body.astype(BF16)
            dst[rows, 0:128] = half
            dst[pl.ds(n * 512, 64), 128:256] = zero.astype(BF16)
            dst[pl.ds(n * 512 + 64, 448), 128:256] = half[:448]
            dst[pl.ds(n * 512, 448), 256:384] = half[64:]
            dst[pl.ds(n * 512 + 448, 64), 256:384] = zero.astype(BF16)
            cube = body.reshape(8, 8, 8, 128)
            low = jnp.concatenate([plate, cube[:, :7]], axis=1)
            dst[rows, 384:512] = low.reshape(512, 128).astype(BF16)
            high = jnp.concatenate([cube[:, 1:], plate], axis=1)
            dst[rows, 512:640] = high.reshape(512, 128).astype(BF16)
            s32[...] = a32[pl.ds(base - 1, 512), :]
            s32[pl.ds(0, 64, stride=8), :] = zero
            dst[rows, 640:768] = s32[...].astype(BF16)
            s32[...] = a32[pl.ds(base + 1, 512), :]
            s32[pl.ds(7, 64, stride=8), :] = zero
            dst[rows, 768:896] = s32[...].astype(BF16)

    def add_face(target, n, f, term):
        base = n * 512
        if f == 0:
            target[pl.ds(base, 64), :] += term
        elif f == 1:
            target[pl.ds(base + 448, 64), :] += term
        elif f < 4:
            term = natural(term)
            for i in range(8):
                target[pl.ds(base + i * 64 + (f - 2) * 56, 8), :] += term[i * 8 : i * 8 + 8]
        else:
            rows = pl.ds(base + (f - 4) * 7, 64, stride=8)
            target[rows, :] = target[rows, :] + natural(term)

    def add_faces(target, slab, w):
        for f in range(6):
            both = jnp.concatenate([slab(f), slab(6 + f)], axis=0)
            term = dot(both, w[pl.ds((f + 1) * 128, 128), :])
            add_face(target, 0, f, term[:64])
            add_face(target, 1, f, term[64:])

    def product(target, cols, w):
        def rows_of(r):
            rows = pl.ds(r, 256)
            target[rows, :] = dot(cols[rows, :], w[...])

        chunks(4, 256, rows_of)

    def back_rows(r, up, gain, xh, sl, rs):
        rows = pl.ds(r, 128)
        xhat = xh[rows, :]
        dt = up * sl[rows, :]
        d = dt * gain
        mean_d = jnp.mean(d, axis=-1, keepdims=True)
        mean_dx = jnp.mean(d * xhat, axis=-1, keepdims=True)
        return rs[rows, :] * (d - mean_d - xhat * mean_dx), dt * xhat

    def pre_rows(v, r, gain, xh, sl, rs):
        rows = pl.ds(r, 128)
        xhat, inv = norm(v)
        a, slope = silu_parts(xhat * gain)
        xh[rows, :] = xhat
        sl[rows, :] = slope
        rs[rows, :] = jnp.broadcast_to(inv, (128, 128))
        return a

    alive = [live_s[n].astype(F32) for n in range(2)]

    step_id = lax.broadcasted_iota(jnp.int32, (8, 128), 0)
    lane_id = lax.broadcasted_iota(jnp.int32, (8, 128), 1)
    in_x = lane_id % 8
    target_id = (
        ((xi + in_x // 2) % XD) * (2 * ZD) + ((zi + step_id) % ZD) * 2 + (ci + in_x % 2) % 2
    )
    codes = jnp.full((8, 128), -1, jnp.int32)
    for e in range(64):
        codes = jnp.where(target_id == e, send_s[e], codes)
    back = jnp.full((8, 128), -1, jnp.int32)
    for q in range(12):
        back = jnp.where(target_id == recv_s[q // 6, q % 6], q, back)
    chosen = jnp.where(lane_id < 8, codes, back)
    tbl[0] = chosen + 2 * (chosen >= 6).astype(jnp.int32)

    wait(x_ref, ld_sem.at[0])
    a32[pl.ds(LO, 1024), :] = x_ref[...].astype(F32)
    faces(0)
    pl.semaphore_wait(barrier, 24)
    for o in range(1, ZD):
        push(tbl.at[0], tbl.at[o], t_sem.at[0], t_sem.at[1], z_dev(o))
    forward(0, 0)

    lane = lax.broadcasted_iota(jnp.int32, (64, 128), 1)
    line = lax.broadcasted_iota(jnp.int32, (64, 128), 0)
    across = jnp.full((8, 128), 99, jnp.int32)
    for e in range(64):
        across = jnp.where(lane_id == e, send_s[e], across)
        col[pl.ds(e, 1), :] = jnp.full((1, 128), send_s[e], jnp.int32)
    across = jnp.broadcast_to(across[0:1], (64, 128))
    down = col[...]
    ahead = (down < across) | ((down == across) & (line < lane))
    rank = jnp.sum(ahead.astype(jnp.int32), axis=0, keepdims=True)
    value = position(jnp.minimum(lane, 63)) + 64 * (jnp.minimum(across, 15) + 1)
    sorted_values = jnp.sum(
        jnp.where((rank == line) & (lane < 64), value, 0), axis=1, keepdims=True
    )
    ordv[pl.ds(0, 64), :] = jnp.broadcast_to(sorted_values, (64, 128))
    below = jnp.sum((across < line).astype(jnp.int32), axis=1, keepdims=True)
    ordv[pl.ds(64, 16), :] = jnp.broadcast_to(below, (64, 128))[:16]
    pltpu.make_async_copy(ordv, ord_s, ld_sem.at[7]).start()

    wait(cot_ref, ld_sem.at[1])
    for n in range(2):
        a32[pl.ds(LO + n * 512, 512), :] = cot_ref[pl.ds(n * 512, 512), :].astype(F32) * alive[n]
    faces(1)
    columns(v7)
    wait(tbl.at[pl.ds(1, 7)], t_sem.at[1])
    codes_in = pltpu.make_async_copy(tbl, tbl_s, ld_sem.at[6])
    codes_in.start()
    codes_in.wait()
    hop(0, 1)

    wait(gains.at[0], ld_sem.at[4])
    wait(gains.at[1], ld_sem.at[5])
    gain1 = gains[0]
    gain2 = gains[1]

    def act_one(r):
        a = pre_rows(x_ref[pl.ds(r, 128), :].astype(F32), r, gain1, xh1, sl1, rs1)
        a32[pl.ds(LO + r, 128), :] = rounded(a)

    chunks(8, 128, act_one)
    hop(0, 2)
    hop(1, 0)
    columns(u7)
    wait(w1_ref, ld_sem.at[2])
    wait(w2_ref, ld_sem.at[3])
    product(acc, u7, w1_ref)
    hop(0, 3)
    for t in range(7):
        src = pl.ds(SWAP[t] * 128, 128)
        wt1[pl.ds(t * 128, 128), :] = w1_ref[src, :].astype(F32).T.astype(BF16)
        wt2[pl.ds(t * 128, 128), :] = w2_ref[src, :].astype(F32).T.astype(BF16)
    product(acc2, v7, wt2)
    hop(1, 1)

    arrived(0)

    def halo_one(q, carry):
        xhat, _ = norm(take_halo(0, q))
        act, slope = silu_parts(xhat * gain1)
        hal[q] = act.astype(BF16)
        hald[q] = slope * xhat
        return carry

    lax.fori_loop(0, 12, halo_one, 0, unroll=UNH)
    add_faces(acc, lambda q: hal[q], w1_ref)

    def hidden_rows(r):
        rows = pl.ds(r, 128)
        a = pre_rows(rounded(acc[rows, :]), r, gain2, xh2, sl2, rs2).astype(BF16)
        act2[rows, :] = a
        a32[pl.ds(LO + r, 128), :] = a.astype(F32)

    chunks(8, 128, hidden_rows)
    faces(2)
    hop(1, 2)
    hop(2, 0)

    hop(1, 3)
    hop(2, 1)
    pltpu.make_async_copy(ordv, ord_s, ld_sem.at[7]).wait()
    returns(1)
    add_faces(acc2, lambda q: ret[q].astype(BF16), wt2)
    wg[pl.ds(1792, 256), :] = jnp.zeros((256, 128), F32)

    def grad_hidden_rows(r):
        grad, per = back_rows(r, acc2[pl.ds(r, 128), :], gain2, xh2, sl2, rs2)
        a32[pl.ds(LO + r, 128), :] = rounded(grad)
        wg[pl.ds(1793, 1), :] += jnp.sum(per, axis=0, keepdims=True)

    chunks(8, 128, grad_hidden_rows)
    faces(3)
    hop(3, 0)
    hop(2, 2)

    def slabs(pay, f):
        return gath[pay][0][:, f].reshape(128, 128)

    a2 = act2[...]
    for t in range(7):
        total = dot_t(a2, v7[:, t * 128 : t * 128 + 128])
        if t > 0:
            r2 = jnp.concatenate([ret[t - 1], ret[t + 5]], axis=0).astype(BF16)
            total = total + dot_t(slabs(2, t - 1), r2)
        wg[pl.ds(896 + SWAP[t] * 128, 128), :] = total
    gh = a32[pl.ds(LO, 1024), :].astype(BF16)
    for t in range(7):
        total = dot_t(u7[:, t * 128 : t * 128 + 128], gh)
        if t > 0:
            h2 = jnp.concatenate([hal[t - 1], hal[t + 5]], axis=0)
            total = total + dot_t(h2, slabs(3, t - 1))
        wg[pl.ds(t * 128, 128), :] = total

    columns(v7)
    product(acc2, v7, wt1)

    def gain_rows(r):
        rows = pl.ds(r, 128)
        per = acc2[rows, :] * sl1[rows, :] * xh1[rows, :]
        wg[pl.ds(1792, 1), :] += jnp.sum(per, axis=0, keepdims=True)

    chunks(8, 128, gain_rows)
    for f in range(6):
        both = dot(slabs(3, f), wt1[pl.ds(SWAP[f + 1] * 128, 128), :])
        slope = jnp.concatenate([hald[f], hald[6 + f]], axis=0)
        wg[pl.ds(1792, 1), :] += jnp.sum(rounded(both) * slope, axis=0, keepdims=True)

    half = pl.multiple_of(ci * 1024, 1024)
    other = pl.multiple_of((1 - ci) * 1024, 1024)
    mine = pl.multiple_of(half + y * 256, 256)
    ac_out[...] = wg[pl.ds(other, 1024), :].astype(BF16)
    push(ac_out, ac_in, ar_sem.at[3, 0], ar_sem.at[3, 1], row_dev(1))

    wait(ac_in, ar_sem.at[3, 1])
    wg[pl.ds(half, 1024), :] += ac_in[...].astype(F32)
    for o in range(1, YD):
        start = pl.multiple_of(half + (y + o) % YD * 256, 256)
        ay_out[o] = wg[pl.ds(start, 256), :].astype(BF16)
        push(ay_out.at[o], ay_in.at[o], ar_sem.at[0, 0], ar_sem.at[0, 1], y_dev(o))
    hop(3, 1)
    hop(2, 3)

    a32[pl.ds(LO, 1024), :] = act2[...].astype(F32)
    columns(u7)
    product(acc, u7, w2_ref)

    wait(ay_in.at[pl.ds(1, 3)], ar_sem.at[0, 1])
    partial = wg[pl.ds(mine, 256), :]
    for o in range(1, YD):
        partial = partial + ay_in[o].astype(F32)
    wg[pl.ds(mine, 256), :] = partial
    for o in range(1, XD):
        start = pl.multiple_of(mine + ((xi + o) % XD) * 64, 64)
        ax_out[o] = wg[pl.ds(start, 64), :].astype(BF16)
        push(ax_out.at[o], ax_in.at[o], ar_sem.at[1, 0], ar_sem.at[1, 1], x_dev(o))

    arrived(2)
    add_faces(acc, lambda q: take_halo(2, q).astype(BF16), w2_ref)
    for n in range(2):
        rows = pl.ds(n * 512, 512)
        out_ref[rows, :] = ((x_ref[rows, :].astype(F32) + acc[rows, :]) * alive[n]).astype(BF16)


    wait(ax_in.at[pl.ds(1, 3)], ar_sem.at[1, 1])
    mine_x = pl.multiple_of(mine + xi * 64, 64)
    partial = wg[pl.ds(mine_x, 64), :]
    for o in range(1, XD):
        partial = partial + ax_in[o].astype(F32)
    az[0] = partial.astype(BF16)
    for o in range(1, ZD):
        push(az.at[0], az.at[o], ar_sem.at[2, 0], ar_sem.at[2, 1], z_dev(o))

    hop(3, 2)
    wait(az.at[pl.ds(1, 7)], ar_sem.at[2, 1])
    total = jnp.zeros((64, 128), F32)
    for k in range(ZD):
        total = total + az[(zi - k + ZD) % ZD].astype(F32)
    fin[pl.ds(mine_x, 64), :] = (total * scale).astype(BF16)
    piece = fin.at[pl.ds(mine_x, 64)]
    for o in range(1, XD):
        push(piece, piece, ag_sem.at[0, 0, o], ag_sem.at[0, 1, o], x_dev(o))

    hop(3, 3)

    def gather_y():
        for o in range(1, XD):
            start = pl.multiple_of(mine + ((xi - o + XD) % XD) * 64, 64)
            wait(fin.at[pl.ds(start, 64)], ag_sem.at[0, 1, o])
        piece = fin.at[pl.ds(mine, 256)]
        for o in range(1, YD):
            push(piece, piece, ag_sem.at[1, 0, o], ag_sem.at[1, 1, o], y_dev(o))

    gather_y()
    returns(3)
    for o in range(1, YD):
        start = pl.multiple_of(half + (y - o + YD) % YD * 256, 256)
        wait(fin.at[pl.ds(start, 256)], ag_sem.at[1, 1, o])
    piece = fin.at[pl.ds(half, 1024)]
    push(piece, piece, ag_sem.at[2, 0, 0], ag_sem.at[2, 1, 0], row_dev(1))
    add_faces(acc2, lambda q: ret[q].astype(BF16), wt1)
    for n in range(2):

        def grad_rows(i, n=n):
            r = pl.multiple_of(n * 512 + i, 128)
            rows = pl.ds(r, 128)
            grad, _ = back_rows(r, acc2[rows, :], gain1, xh1, sl1, rs1)
            gf_ref[rows, :] = (cot_ref[rows, :].astype(F32) * alive[n] + grad).astype(BF16)

        chunks(4, 128, grad_rows)

    wait(fin.at[pl.ds(other, 1024)], ag_sem.at[2, 1, 0])
    gw1_ref[...] = fin[pl.ds(0, 896), :].astype(F32)
    gw2_ref[...] = fin[pl.ds(896, 896), :].astype(F32)
    last = fin[pl.ds(1792, 16), :].astype(F32)
    gg1_ref[...] = last[0:1]
    gg2_ref[...] = last[1:2]

    for pay in range(4):
        for o in (1, 2, 3, 5, 6, 7):
            for k in range(2):
                wait(part(pay, o, k), ring_send.at[pay, o, k])
        for group in range(4):
            wait(outb.at[(pay, *flying(group))], x_send.at[pay, group])
    wait(tbl.at[pl.ds(1, 7)], t_sem.at[0])
    wait(ac_out, ar_sem.at[3, 0])
    wait(ay_out.at[pl.ds(1, 3)], ar_sem.at[0, 0])
    wait(ax_out.at[pl.ds(1, 3)], ar_sem.at[1, 0])
    wait(az.at[pl.ds(1, 7)], ar_sem.at[2, 0])
    for o in range(1, XD):
        wait(fin.at[pl.ds(mine_x, 64)], ag_sem.at[0, 0, o])
    for o in range(1, YD):
        wait(fin.at[pl.ds(mine, 256)], ag_sem.at[1, 0, o])
    wait(fin.at[pl.ds(half, 1024)], ag_sem.at[2, 0, 0])


def hand_over(*refs):
    sems = refs[12]
    stores = [pltpu.make_async_copy(refs[i], refs[6 + i], sems.at[i]) for i in range(6)]
    for store in stores:
        store.start()
    for store in stores:
        store.wait()


def shards(
    features, gain_one, weight_one, gain_two, weight_two, live, send_index, recv_index, cotangent
):
    scale = 1.0 / math.sqrt(
        features.shape[1] * features.shape[2] * lax.axis_size("shape") * lax.axis_size("space")
    )
    rows = 1024
    smem = pl.BlockSpec(memory_space=pltpu.SMEM)
    hbm = pl.BlockSpec(memory_space=pltpu.HBM)
    vmem = pl.BlockSpec(memory_space=pltpu.VMEM)
    shapes = [
        jax.ShapeDtypeStruct((rows, 128), BF16),
        jax.ShapeDtypeStruct((rows, 128), BF16),
        jax.ShapeDtypeStruct((896, 128), F32),
        jax.ShapeDtypeStruct((896, 128), F32),
        jax.ShapeDtypeStruct((1, 128), F32),
        jax.ShapeDtypeStruct((1, 128), F32),
    ]
    results = pl.pallas_call(
        functools.partial(kernel, scale),
        out_shape=[pltpu.VMEM(s.shape, s.dtype) for s in shapes],
        in_specs=[smem] * 3 + [hbm] * 6,
        out_specs=[vmem] * 6,
        scratch_shapes=[
            *[pltpu.VMEM((2, 6, 64, 128), BF16)] * 32,
            *[pltpu.VMEM((8, 8, 64, 128), BF16)] * 4,
            pltpu.VMEM((4, 8, 8, 64, 128), BF16),
            pltpu.VMEM((8, 8, 128), jnp.int32),
            pltpu.SMEM((8, 8, 128), jnp.int32),
            pltpu.VMEM((80, 128), jnp.int32),
            pltpu.SMEM((80, 128), jnp.int32),
            pltpu.VMEM((64, 64, 128), F32),
            pltpu.VMEM((64, 128), jnp.int32),
            pltpu.VMEM((rows, 128), BF16),
            pltpu.VMEM((rows, 128), BF16),
            pltpu.VMEM((896, 128), BF16),
            pltpu.VMEM((896, 128), BF16),
            pltpu.VMEM((2, 1, 128), F32),
            pltpu.VMEM((1040, 128), F32),
            pltpu.VMEM((512, 128), F32),
            pltpu.VMEM((128, 128), F32),
            pltpu.VMEM((rows, 896), BF16),
            pltpu.VMEM((rows, 896), BF16),
            pltpu.VMEM((rows, 128), BF16),
            *[pltpu.VMEM((rows, 128), F32)] * 8,
            pltpu.VMEM((12, 64, 128), BF16),
            pltpu.VMEM((12, 64, 128), F32),
            pltpu.VMEM((12, 64, 128), F32),
            pltpu.VMEM((896, 128), BF16),
            pltpu.VMEM((896, 128), BF16),
            pltpu.VMEM((2048, 128), F32),
            pltpu.VMEM((2048, 128), BF16),
            pltpu.VMEM((1024, 128), BF16),
            pltpu.VMEM((1024, 128), BF16),
            pltpu.VMEM((4, 256, 128), BF16),
            pltpu.VMEM((4, 256, 128), BF16),
            pltpu.VMEM((4, 64, 128), BF16),
            pltpu.VMEM((4, 64, 128), BF16),
            pltpu.VMEM((8, 64, 128), BF16),
            pltpu.SemaphoreType.DMA((4, 8, 2)),
            pltpu.SemaphoreType.DMA((4, 8, 2)),
            pltpu.SemaphoreType.DMA((4, 4)),
            pltpu.SemaphoreType.DMA((4, 4)),
            pltpu.SemaphoreType.DMA((2,)),
            pltpu.SemaphoreType.DMA((4, 2)),
            pltpu.SemaphoreType.DMA((3, 2, 4)),
            pltpu.SemaphoreType.DMA((8,)),
        ],
        compiler_params=pltpu.CompilerParams(
            collective_id=0, has_side_effects=True, vmem_limit_bytes=56 * 1024 * 1024
        ),
    )(
        send_index.reshape(64),
        recv_index.reshape(2, 6),
        live.reshape(2),
        features.reshape(rows, 128),
        gain_one.reshape(1, 128),
        weight_one.reshape(896, 128),
        gain_two.reshape(1, 128),
        weight_two.reshape(896, 128),
        cotangent.reshape(rows, 128),
    )
    out, grad, w1, w2, g1, g2 = pl.pallas_call(
        hand_over,
        out_shape=shapes,
        in_specs=[vmem] * 6,
        out_specs=[hbm] * 6,
        scratch_shapes=[pltpu.SemaphoreType.DMA((6,))],
    )(*[pltpu.with_memory_space_constraint(r, pltpu.VMEM) for r in results])
    return (
        out.reshape(features.shape),
        grad.reshape(features.shape),
        w1.reshape(7, 128, 128),
        w2.reshape(7, 128, 128),
        g1.reshape(128),
        g2.reshape(128),
    )


def solution(mesh):
    bricks = P("shape", "space", None, None)
    in_specs = (
        bricks,
        P(),
        P(),
        P(),
        P(),
        P("shape", "space"),
        bricks,
        P("shape", "space", None),
        bricks,
    )
    out_specs = (bricks, bricks, P(), P(), P(), P())
    return jax.shard_map(shards, mesh=mesh, in_specs=in_specs, out_specs=out_specs, check_vma=False)
```

```python
import functools
import math

import jax
import jax.numpy as jnp
from jax import lax
from jax.experimental import pallas as pl
from jax.experimental.pallas import tpu as pltpu
from jax.sharding import PartitionSpec as P

MESH = pl.DeviceIdType.MESH
F32 = jnp.float32
BF16 = jnp.bfloat16
EPS = 1e-05
SWAP = (0, 2, 1, 4, 3, 6, 5)
XD, ZD, YD = 4, 8, 4
LO = 8
UNH = 4
UNC = 4
UNP = 4
POS = (0, 1, 3, 5, 7, 6, 4, 2)
GROUPS = ((0, 3), (3, 2), (5, 2), (7, 1))


def norm(v):
    c = v - jnp.mean(v, axis=-1, keepdims=True)
    r = lax.rsqrt(jnp.mean(c * c, axis=-1, keepdims=True) + EPS)
    return c * r, r


def silu_parts(t):
    s = 0.5 * jnp.tanh(0.5 * t) + 0.5
    return t * s, s * (1.0 + t * (1.0 - s))


def rounded(v):
    return v.astype(BF16).astype(F32)


def dot(a, b):
    return jnp.dot(a, b, preferred_element_type=F32)


def dot_t(a, b):
    return lax.dot_general(a, b, (((0,), (0,)), ((), ())), preferred_element_type=F32)


def kernel(
    scale,
    send_s,
    recv_s,
    live_s,
    x_hbm,
    g1_hbm,
    w1_hbm,
    g2_hbm,
    w2_hbm,
    cot_hbm,
    out_ref,
    gf_ref,
    gw1_ref,
    gw2_ref,
    gg1_ref,
    gg2_ref,
    *scratch,
):
    gath = [scratch[i * 8 : i * 8 + 8] for i in range(4)]
    inb = scratch[32:36]
    (
        outb,
        tbl,
        tbl_s,
        ordv,
        ord_s,
        seg,
        col,
        x_ref,
        cot_ref,
        w1_ref,
        w2_ref,
        gains,
        a32,
        s32,
        e32,
        u7,
        v7,
        act2,
        acc,
        acc2,
        xh1,
        sl1,
        rs1,
        xh2,
        sl2,
        rs2,
        hal,
        hald,
        ret,
        wt1,
        wt2,
        wg,
        fin,
        ac_out,
        ac_in,
        ay_out,
        ay_in,
        ax_out,
        ax_in,
        az,
        ring_send,
        ring_recv,
        x_send,
        x_recv,
        t_sem,
        ar_sem,
        ag_sem,
        ld_sem,
    ) = scratch[36:]
    y = lax.axis_index("shape")
    sp = lax.axis_index("space")
    xi = sp // 16
    zi = (sp // 2) % ZD
    ci = sp % 2

    def dev(yy, xx, zz, cc):
        return (yy, (xx * ZD + zz) * 2 + cc)

    def z_dev(o):
        return dev(y, xi, (zi + o) % ZD, ci)

    def row_dev(l, step=0):
        return dev(y, (xi + l // 2) % XD, (zi + step + ZD) % ZD, (ci + l % 2) % 2)

    def row_source(l, step):
        return dev(y, (xi - l // 2 + XD) % XD, (zi + step + ZD) % ZD, (ci + l % 2) % 2)

    def x_dev(o):
        return dev(y, (xi + o) % XD, zi, ci)

    def y_dev(o):
        return dev((y + o) % YD, xi, zi, ci)

    barrier = pltpu.get_barrier_semaphore()

    def greet(target):
        pl.semaphore_signal(barrier, inc=1, device_id=target, device_id_type=MESH)

    for o in range(1, ZD):
        greet(z_dev(o))
    for l in range(1, 8):
        greet(row_dev(l))
    for o in range(1, YD):
        greet(y_dev(o))
    for l in range(1, 4):
        greet(row_source(l, -1))
    for l in range(4, 8):
        greet(row_source(l, 1))

    def load(src, dst, i):
        pltpu.make_async_copy(src, dst, ld_sem.at[i]).start()

    load(x_hbm, x_ref, 0)
    load(cot_hbm, cot_ref, 1)
    load(w1_hbm, w1_ref, 2)
    load(w2_hbm, w2_ref, 3)
    load(g1_hbm, gains.at[0], 4)
    load(g2_hbm, gains.at[1], 5)

    def push(src, dst, ssem, rsem, target):
        pltpu.make_async_remote_copy(
            src_ref=src,
            dst_ref=dst,
            send_sem=ssem,
            recv_sem=rsem,
            device_id=target,
            device_id_type=MESH,
        ).start()

    def wait(ref, sem):
        pltpu.make_async_copy(ref, ref, sem).wait()

    def part(pay, slot, k):
        if k == 0:
            return gath[pay][slot].at[:, pl.ds(0, 2)]
        return gath[pay][slot].at[:, pl.ds(2, 4), pl.ds(0, 48)]

    def ring(pay, src, dst, k, step):
        push(
            part(pay, src, k),
            part(pay, dst, k),
            ring_send.at[pay, dst, k],
            ring_recv.at[pay, dst, k],
            z_dev(step),
        )

    def forward(pay, h):
        for k in range(2):
            for src, dst, step in ((h, h + 1, 1), ((ZD - h) % ZD, ZD - 1 - h, ZD - 1)):
                if h > 0:
                    wait(part(pay, src, k), ring_recv.at[pay, src, k])
                if h < 3:
                    ring(pay, src, dst, k, step)

    def fill(pay, slot):
        g = gath[pay][slot]
        for n in range(2):
            e32[...] = g[n, 0:2].reshape(128, 128).astype(F32)
            g[n, 2, 48:64] = jnp.concatenate([e32[0:8], e32[64:72]], axis=0).astype(BF16)
            g[n, 3, 48:64] = jnp.concatenate([e32[56:64], e32[120:128]], axis=0).astype(BF16)
            g[n, 4, 48:64] = e32[pl.ds(0, 16, stride=8), :].astype(BF16)
            g[n, 5, 48:64] = e32[pl.ds(7, 16, stride=8), :].astype(BF16)

    def pick(pay, slot, o, l):
        code = jnp.maximum(tbl_s[slot, o, l + 8 * (pay % 2)], 0)
        slab = gath[pay][slot][code // 8, code % 8]
        if l == 0 and o == slot:
            inb[pay][0, POS[o]] = slab
        else:
            outb[pay, l, POS[o]] = slab

    def deliver(pay, group, l, step):
        first, count = GROUPS[group]
        push(
            outb.at[pay, l, pl.ds(first, count)],
            inb[pay].at[l, pl.ds(first, count)],
            x_send.at[pay, group],
            x_recv.at[pay, group],
            row_dev(l, step),
        )

    def select(pay, h):
        if h == 3:
            for l in range(4):
                pick(pay, 3, 4, l)
                deliver(pay, 3, l, 1)
            for l in range(4, 8):
                pick(pay, 5, 4, l)
                deliver(pay, 3, l, -1)
        for l in (4, 5, 2, 3, 6, 7, 1, 0):
            for o in ((0, 1, 7), (2, 6), (3, 5))[h - 1]:
                pick(pay, o, o, l)
            if l > 0:
                deliver(pay, h - 1, l, 0)

    def flying(group):
        first, count = GROUPS[group]
        return (pl.ds(0, 8) if group == 3 else pl.ds(1, 7)), pl.ds(first, count)

    def arrived(pay):
        for group in range(4):
            wait(inb[pay].at[flying(group)], x_recv.at[pay, group])

    def hop(pay, h):
        forward(pay, h)
        if h > 0:
            fill(pay, h)
            fill(pay, ZD - h)
            select(pay, h)

    def returns(pay):
        arrived(pay)

        def one(k, carry):
            total, before = carry
            v = ord_s[k, 0]
            code, at = v // 64, v % 64
            total = total * (code == before).astype(F32) + inb[pay][at // 8, at % 8].astype(F32)
            seg[k] = total
            return total, code

        lax.fori_loop(0, 64, one, (jnp.zeros((64, 128), F32), jnp.int32(-1)), unroll=8)

        def pickup(q, carry):
            start, end = ord_s[64 + q, 0], ord_s[65 + q, 0]
            ret[q] = seg[jnp.maximum(end - 1, 0)] * (end > start).astype(F32)
            return carry

        lax.fori_loop(0, 12, pickup, 0, unroll=4)

    def position(r):
        o = (zi - (r // 2) % ZD + ZD) % ZD
        l = ((xi - r // 16 + XD) % XD) * 2 + (ci + r % 2) % 2
        near = jnp.where(o < 4, jnp.maximum(2 * o - 1, 0), jnp.where(o > 4, 16 - 2 * o, 7))
        return l * 8 + near

    def take_halo(pay, q):
        r = recv_s[q // 6, q % 6]
        at = position(jnp.maximum(r, 0))
        return inb[pay][at // 8, at % 8].astype(F32) * (r >= 0).astype(F32)

    def chunks(n, size, body):
        def step(i, carry):
            body(pl.multiple_of(i * size, size))
            return carry

        lax.fori_loop(0, n, step, 0, unroll=UNC if size == 128 else UNP)

    def ordered(v):
        v = v.reshape(8, 8, 128)
        return jnp.concatenate([v[1:7], v[0:1], v[7:8]], axis=0).reshape(64, 128)

    def natural(v):
        v = v.reshape(8, 8, 128)
        return jnp.concatenate([v[6:7], v[0:6], v[7:8]], axis=0).reshape(64, 128)

    def faces(pay):
        g = gath[pay][0]
        for n in range(2):
            base = LO + n * 512
            cube = a32[pl.ds(base, 512), :].reshape(8, 8, 8, 128)
            g[n, 0] = a32[pl.ds(base, 64), :].astype(BF16)
            g[n, 1] = a32[pl.ds(base + 448, 64), :].astype(BF16)
            g[n, 2] = ordered(cube[:, 0]).astype(BF16)
            g[n, 3] = ordered(cube[:, 7]).astype(BF16)
            g[n, 4] = ordered(a32[pl.ds(base, 64, stride=8), :]).astype(BF16)
            g[n, 5] = ordered(a32[pl.ds(base + 7, 64, stride=8), :]).astype(BF16)

    def columns(dst):
        zero = jnp.zeros((64, 128), F32)
        plate = jnp.zeros((8, 1, 8, 128), F32)
        for n in range(2):
            base = LO + n * 512
            rows = pl.ds(n * 512, 512)
            body = a32[pl.ds(base, 512), :]
            half = body.astype(BF16)
            dst[rows, 0:128] = half
            dst[pl.ds(n * 512, 64), 128:256] = zero.astype(BF16)
            dst[pl.ds(n * 512 + 64, 448), 128:256] = half[:448]
            dst[pl.ds(n * 512, 448), 256:384] = half[64:]
            dst[pl.ds(n * 512 + 448, 64), 256:384] = zero.astype(BF16)
            cube = body.reshape(8, 8, 8, 128)
            low = jnp.concatenate([plate, cube[:, :7]], axis=1)
            dst[rows, 384:512] = low.reshape(512, 128).astype(BF16)
            high = jnp.concatenate([cube[:, 1:], plate], axis=1)
            dst[rows, 512:640] = high.reshape(512, 128).astype(BF16)
            s32[...] = a32[pl.ds(base - 1, 512), :]
            s32[pl.ds(0, 64, stride=8), :] = zero
            dst[rows, 640:768] = s32[...].astype(BF16)
            s32[...] = a32[pl.ds(base + 1, 512), :]
            s32[pl.ds(7, 64, stride=8), :] = zero
            dst[rows, 768:896] = s32[...].astype(BF16)

    def add_face(target, n, f, term):
        base = n * 512
        if f == 0:
            target[pl.ds(base, 64), :] += term
        elif f == 1:
            target[pl.ds(base + 448, 64), :] += term
        elif f < 4:
            term = natural(term)
            for i in range(8):
                target[pl.ds(base + i * 64 + (f - 2) * 56, 8), :] += term[i * 8 : i * 8 + 8]
        else:
            rows = pl.ds(base + (f - 4) * 7, 64, stride=8)
            target[rows, :] = target[rows, :] + natural(term)

    def add_faces(target, slab, w):
        for f in range(6):
            both = jnp.concatenate([slab(f), slab(6 + f)], axis=0)
            term = dot(both, w[pl.ds((f + 1) * 128, 128), :])
            add_face(target, 0, f, term[:64])
            add_face(target, 1, f, term[64:])

    def product(target, cols, w):
        def rows_of(r):
            rows = pl.ds(r, 256)
            target[rows, :] = dot(cols[rows, :], w[...])

        chunks(4, 256, rows_of)

    def back_rows(r, up, gain, xh, sl, rs):
        rows = pl.ds(r, 128)
        xhat = xh[rows, :]
        dt = up * sl[rows, :]
        d = dt * gain
        mean_d = jnp.mean(d, axis=-1, keepdims=True)
        mean_dx = jnp.mean(d * xhat, axis=-1, keepdims=True)
        return rs[rows, :] * (d - mean_d - xhat * mean_dx), dt * xhat

    def pre_rows(v, r, gain, xh, sl, rs):
        rows = pl.ds(r, 128)
        xhat, inv = norm(v)
        a, slope = silu_parts(xhat * gain)
        xh[rows, :] = xhat
        sl[rows, :] = slope
        rs[rows, :] = jnp.broadcast_to(inv, (128, 128))
        return a

    alive = [live_s[n].astype(F32) for n in range(2)]

    step_id = lax.broadcasted_iota(jnp.int32, (8, 128), 0)
    lane_id = lax.broadcasted_iota(jnp.int32, (8, 128), 1)
    in_x = lane_id % 8
    target_id = (
        ((xi + in_x // 2) % XD) * (2 * ZD) + ((zi + step_id) % ZD) * 2 + (ci + in_x % 2) % 2
    )
    codes = jnp.full((8, 128), -1, jnp.int32)
    for e in range(64):
        codes = jnp.where(target_id == e, send_s[e], codes)
    back = jnp.full((8, 128), -1, jnp.int32)
    for q in range(12):
        back = jnp.where(target_id == recv_s[q // 6, q % 6], q, back)
    chosen = jnp.where(lane_id < 8, codes, back)
    tbl[0] = chosen + 2 * (chosen >= 6).astype(jnp.int32)

    wait(x_ref, ld_sem.at[0])
    a32[pl.ds(LO, 1024), :] = x_ref[...].astype(F32)
    faces(0)
    pl.semaphore_wait(barrier, 24)
    for o in range(1, ZD):
        push(tbl.at[0], tbl.at[o], t_sem.at[0], t_sem.at[1], z_dev(o))
    forward(0, 0)

    lane = lax.broadcasted_iota(jnp.int32, (64, 128), 1)
    line = lax.broadcasted_iota(jnp.int32, (64, 128), 0)
    across = jnp.full((8, 128), 99, jnp.int32)
    for e in range(64):
        across = jnp.where(lane_id == e, send_s[e], across)
        col[pl.ds(e, 1), :] = jnp.full((1, 128), send_s[e], jnp.int32)
    across = jnp.broadcast_to(across[0:1], (64, 128))
    down = col[...]
    ahead = (down < across) | ((down == across) & (line < lane))
    rank = jnp.sum(ahead.astype(jnp.int32), axis=0, keepdims=True)
    value = position(jnp.minimum(lane, 63)) + 64 * (jnp.minimum(across, 15) + 1)
    sorted_values = jnp.sum(
        jnp.where((rank == line) & (lane < 64), value, 0), axis=1, keepdims=True
    )
    ordv[pl.ds(0, 64), :] = jnp.broadcast_to(sorted_values, (64, 128))
    below = jnp.sum((across < line).astype(jnp.int32), axis=1, keepdims=True)
    ordv[pl.ds(64, 16), :] = jnp.broadcast_to(below, (64, 128))[:16]
    pltpu.make_async_copy(ordv, ord_s, ld_sem.at[7]).start()

    wait(cot_ref, ld_sem.at[1])
    for n in range(2):
        a32[pl.ds(LO + n * 512, 512), :] = cot_ref[pl.ds(n * 512, 512), :].astype(F32) * alive[n]
    faces(1)
    columns(v7)
    wait(tbl.at[pl.ds(1, 7)], t_sem.at[1])
    codes_in = pltpu.make_async_copy(tbl, tbl_s, ld_sem.at[6])
    codes_in.start()
    codes_in.wait()
    hop(0, 1)

    wait(gains.at[0], ld_sem.at[4])
    wait(gains.at[1], ld_sem.at[5])
    gain1 = gains[0]
    gain2 = gains[1]

    def act_one(r):
        a = pre_rows(x_ref[pl.ds(r, 128), :].astype(F32), r, gain1, xh1, sl1, rs1)
        a32[pl.ds(LO + r, 128), :] = rounded(a)

    chunks(8, 128, act_one)
    hop(0, 2)
    hop(1, 0)
    columns(u7)
    wait(w1_ref, ld_sem.at[2])
    wait(w2_ref, ld_sem.at[3])
    product(acc, u7, w1_ref)
    hop(0, 3)
    for t in range(7):
        src = pl.ds(SWAP[t] * 128, 128)
        wt1[pl.ds(t * 128, 128), :] = w1_ref[src, :].astype(F32).T.astype(BF16)
        wt2[pl.ds(t * 128, 128), :] = w2_ref[src, :].astype(F32).T.astype(BF16)
    product(acc2, v7, wt2)
    hop(1, 1)

    arrived(0)

    def halo_one(q, carry):
        xhat, _ = norm(take_halo(0, q))
        act, slope = silu_parts(xhat * gain1)
        hal[q] = act.astype(BF16)
        hald[q] = slope * xhat
        return carry

    lax.fori_loop(0, 12, halo_one, 0, unroll=UNH)
    add_faces(acc, lambda q: hal[q], w1_ref)
    hop(1, 2)

    def hidden_rows(r):
        rows = pl.ds(r, 128)
        a = pre_rows(rounded(acc[rows, :]), r, gain2, xh2, sl2, rs2).astype(BF16)
        act2[rows, :] = a
        a32[pl.ds(LO + r, 128), :] = a.astype(F32)

    chunks(8, 128, hidden_rows)
    faces(2)
    hop(2, 0)

    hop(1, 3)
    hop(2, 1)
    pltpu.make_async_copy(ordv, ord_s, ld_sem.at[7]).wait()
    returns(1)
    add_faces(acc2, lambda q: ret[q].astype(BF16), wt2)
    wg[pl.ds(1792, 256), :] = jnp.zeros((256, 128), F32)

    def grad_hidden_rows(r):
        grad, per = back_rows(r, acc2[pl.ds(r, 128), :], gain2, xh2, sl2, rs2)
        a32[pl.ds(LO + r, 128), :] = rounded(grad)
        wg[pl.ds(1793, 1), :] += jnp.sum(per, axis=0, keepdims=True)

    chunks(8, 128, grad_hidden_rows)
    faces(3)
    hop(3, 0)
    hop(2, 2)

    def slabs(pay, f):
        return gath[pay][0][:, f].reshape(128, 128)

    a2 = act2[...]
    for t in range(7):
        total = dot_t(a2, v7[:, t * 128 : t * 128 + 128])
        if t > 0:
            r2 = jnp.concatenate([ret[t - 1], ret[t + 5]], axis=0).astype(BF16)
            total = total + dot_t(slabs(2, t - 1), r2)
        wg[pl.ds(896 + SWAP[t] * 128, 128), :] = total
    gh = a32[pl.ds(LO, 1024), :].astype(BF16)
    for t in range(7):
        total = dot_t(u7[:, t * 128 : t * 128 + 128], gh)
        if t > 0:
            h2 = jnp.concatenate([hal[t - 1], hal[t + 5]], axis=0)
            total = total + dot_t(h2, slabs(3, t - 1))
        wg[pl.ds(t * 128, 128), :] = total

    columns(v7)
    product(acc2, v7, wt1)

    def gain_rows(r):
        rows = pl.ds(r, 128)
        per = acc2[rows, :] * sl1[rows, :] * xh1[rows, :]
        wg[pl.ds(1792, 1), :] += jnp.sum(per, axis=0, keepdims=True)

    chunks(8, 128, gain_rows)
    for f in range(6):
        both = dot(slabs(3, f), wt1[pl.ds(SWAP[f + 1] * 128, 128), :])
        slope = jnp.concatenate([hald[f], hald[6 + f]], axis=0)
        wg[pl.ds(1792, 1), :] += jnp.sum(rounded(both) * slope, axis=0, keepdims=True)

    half = pl.multiple_of(ci * 1024, 1024)
    other = pl.multiple_of((1 - ci) * 1024, 1024)
    mine = pl.multiple_of(half + y * 256, 256)
    ac_out[...] = wg[pl.ds(other, 1024), :].astype(BF16)
    push(ac_out, ac_in, ar_sem.at[3, 0], ar_sem.at[3, 1], row_dev(1))

    wait(ac_in, ar_sem.at[3, 1])
    wg[pl.ds(half, 1024), :] += ac_in[...].astype(F32)
    for o in range(1, YD):
        start = pl.multiple_of(half + (y + o) % YD * 256, 256)
        ay_out[o] = wg[pl.ds(start, 256), :].astype(BF16)
        push(ay_out.at[o], ay_in.at[o], ar_sem.at[0, 0], ar_sem.at[0, 1], y_dev(o))
    hop(3, 1)
    hop(2, 3)

    a32[pl.ds(LO, 1024), :] = act2[...].astype(F32)
    columns(u7)
    product(acc, u7, w2_ref)

    wait(ay_in.at[pl.ds(1, 3)], ar_sem.at[0, 1])
    partial = wg[pl.ds(mine, 256), :]
    for o in range(1, YD):
        partial = partial + ay_in[o].astype(F32)
    wg[pl.ds(mine, 256), :] = partial
    for o in range(1, XD):
        start = pl.multiple_of(mine + ((xi + o) % XD) * 64, 64)
        ax_out[o] = wg[pl.ds(start, 64), :].astype(BF16)
        push(ax_out.at[o], ax_in.at[o], ar_sem.at[1, 0], ar_sem.at[1, 1], x_dev(o))

    arrived(2)
    add_faces(acc, lambda q: take_halo(2, q).astype(BF16), w2_ref)
    for n in range(2):
        rows = pl.ds(n * 512, 512)
        out_ref[rows, :] = ((x_ref[rows, :].astype(F32) + acc[rows, :]) * alive[n]).astype(BF16)


    wait(ax_in.at[pl.ds(1, 3)], ar_sem.at[1, 1])
    mine_x = pl.multiple_of(mine + xi * 64, 64)
    partial = wg[pl.ds(mine_x, 64), :]
    for o in range(1, XD):
        partial = partial + ax_in[o].astype(F32)
    az[0] = partial.astype(BF16)
    for o in range(1, ZD):
        push(az.at[0], az.at[o], ar_sem.at[2, 0], ar_sem.at[2, 1], z_dev(o))

    hop(3, 2)
    wait(az.at[pl.ds(1, 7)], ar_sem.at[2, 1])
    total = jnp.zeros((64, 128), F32)
    for k in range(ZD):
        total = total + az[(zi - k + ZD) % ZD].astype(F32)
    fin[pl.ds(mine_x, 64), :] = (total * scale).astype(BF16)
    piece = fin.at[pl.ds(mine_x, 64)]
    for o in range(1, XD):
        push(piece, piece, ag_sem.at[0, 0, o], ag_sem.at[0, 1, o], x_dev(o))

    hop(3, 3)

    def gather_y():
        for o in range(1, XD):
            start = pl.multiple_of(mine + ((xi - o + XD) % XD) * 64, 64)
            wait(fin.at[pl.ds(start, 64)], ag_sem.at[0, 1, o])
        piece = fin.at[pl.ds(mine, 256)]
        for o in range(1, YD):
            push(piece, piece, ag_sem.at[1, 0, o], ag_sem.at[1, 1, o], y_dev(o))

    gather_y()
    returns(3)
    for o in range(1, YD):
        start = pl.multiple_of(half + (y - o + YD) % YD * 256, 256)
        wait(fin.at[pl.ds(start, 256)], ag_sem.at[1, 1, o])
    piece = fin.at[pl.ds(half, 1024)]
    push(piece, piece, ag_sem.at[2, 0, 0], ag_sem.at[2, 1, 0], row_dev(1))
    add_faces(acc2, lambda q: ret[q].astype(BF16), wt1)
    for n in range(2):

        def grad_rows(i, n=n):
            r = pl.multiple_of(n * 512 + i, 128)
            rows = pl.ds(r, 128)
            grad, _ = back_rows(r, acc2[rows, :], gain1, xh1, sl1, rs1)
            gf_ref[rows, :] = (cot_ref[rows, :].astype(F32) * alive[n] + grad).astype(BF16)

        chunks(4, 128, grad_rows)

    wait(fin.at[pl.ds(other, 1024)], ag_sem.at[2, 1, 0])
    gw1_ref[...] = fin[pl.ds(0, 896), :].astype(F32)
    gw2_ref[...] = fin[pl.ds(896, 896), :].astype(F32)
    last = fin[pl.ds(1792, 16), :].astype(F32)
    gg1_ref[...] = last[0:1]
    gg2_ref[...] = last[1:2]

    for pay in range(4):
        for o in (1, 2, 3, 5, 6, 7):
            for k in range(2):
                wait(part(pay, o, k), ring_send.at[pay, o, k])
        for group in range(4):
            wait(outb.at[(pay, *flying(group))], x_send.at[pay, group])
    wait(tbl.at[pl.ds(1, 7)], t_sem.at[0])
    wait(ac_out, ar_sem.at[3, 0])
    wait(ay_out.at[pl.ds(1, 3)], ar_sem.at[0, 0])
    wait(ax_out.at[pl.ds(1, 3)], ar_sem.at[1, 0])
    wait(az.at[pl.ds(1, 7)], ar_sem.at[2, 0])
    for o in range(1, XD):
        wait(fin.at[pl.ds(mine_x, 64)], ag_sem.at[0, 0, o])
    for o in range(1, YD):
        wait(fin.at[pl.ds(mine, 256)], ag_sem.at[1, 0, o])
    wait(fin.at[pl.ds(half, 1024)], ag_sem.at[2, 0, 0])


def hand_over(*refs):
    sems = refs[12]
    stores = [pltpu.make_async_copy(refs[i], refs[6 + i], sems.at[i]) for i in range(6)]
    for store in stores:
        store.start()
    for store in stores:
        store.wait()


def shards(
    features, gain_one, weight_one, gain_two, weight_two, live, send_index, recv_index, cotangent
):
    scale = 1.0 / math.sqrt(
        features.shape[1] * features.shape[2] * lax.axis_size("shape") * lax.axis_size("space")
    )
    rows = 1024
    smem = pl.BlockSpec(memory_space=pltpu.SMEM)
    hbm = pl.BlockSpec(memory_space=pltpu.HBM)
    vmem = pl.BlockSpec(memory_space=pltpu.VMEM)
    shapes = [
        jax.ShapeDtypeStruct((rows, 128), BF16),
        jax.ShapeDtypeStruct((rows, 128), BF16),
        jax.ShapeDtypeStruct((896, 128), F32),
        jax.ShapeDtypeStruct((896, 128), F32),
        jax.ShapeDtypeStruct((1, 128), F32),
        jax.ShapeDtypeStruct((1, 128), F32),
    ]
    results = pl.pallas_call(
        functools.partial(kernel, scale),
        out_shape=[pltpu.VMEM(s.shape, s.dtype) for s in shapes],
        in_specs=[smem] * 3 + [hbm] * 6,
        out_specs=[vmem] * 6,
        scratch_shapes=[
            *[pltpu.VMEM((2, 6, 64, 128), BF16)] * 32,
            *[pltpu.VMEM((8, 8, 64, 128), BF16)] * 4,
            pltpu.VMEM((4, 8, 8, 64, 128), BF16),
            pltpu.VMEM((8, 8, 128), jnp.int32),
            pltpu.SMEM((8, 8, 128), jnp.int32),
            pltpu.VMEM((80, 128), jnp.int32),
            pltpu.SMEM((80, 128), jnp.int32),
            pltpu.VMEM((64, 64, 128), F32),
            pltpu.VMEM((64, 128), jnp.int32),
            pltpu.VMEM((rows, 128), BF16),
            pltpu.VMEM((rows, 128), BF16),
            pltpu.VMEM((896, 128), BF16),
            pltpu.VMEM((896, 128), BF16),
            pltpu.VMEM((2, 1, 128), F32),
            pltpu.VMEM((1040, 128), F32),
            pltpu.VMEM((512, 128), F32),
            pltpu.VMEM((128, 128), F32),
            pltpu.VMEM((rows, 896), BF16),
            pltpu.VMEM((rows, 896), BF16),
            pltpu.VMEM((rows, 128), BF16),
            *[pltpu.VMEM((rows, 128), F32)] * 8,
            pltpu.VMEM((12, 64, 128), BF16),
            pltpu.VMEM((12, 64, 128), F32),
            pltpu.VMEM((12, 64, 128), F32),
            pltpu.VMEM((896, 128), BF16),
            pltpu.VMEM((896, 128), BF16),
            pltpu.VMEM((2048, 128), F32),
            pltpu.VMEM((2048, 128), BF16),
            pltpu.VMEM((1024, 128), BF16),
            pltpu.VMEM((1024, 128), BF16),
            pltpu.VMEM((4, 256, 128), BF16),
            pltpu.VMEM((4, 256, 128), BF16),
            pltpu.VMEM((4, 64, 128), BF16),
            pltpu.VMEM((4, 64, 128), BF16),
            pltpu.VMEM((8, 64, 128), BF16),
            pltpu.SemaphoreType.DMA((4, 8, 2)),
            pltpu.SemaphoreType.DMA((4, 8, 2)),
            pltpu.SemaphoreType.DMA((4, 4)),
            pltpu.SemaphoreType.DMA((4, 4)),
            pltpu.SemaphoreType.DMA((2,)),
            pltpu.SemaphoreType.DMA((4, 2)),
            pltpu.SemaphoreType.DMA((3, 2, 4)),
            pltpu.SemaphoreType.DMA((8,)),
        ],
        compiler_params=pltpu.CompilerParams(
            collective_id=0, has_side_effects=True, vmem_limit_bytes=56 * 1024 * 1024
        ),
    )(
        send_index.reshape(64),
        recv_index.reshape(2, 6),
        live.reshape(2),
        features.reshape(rows, 128),
        gain_one.reshape(1, 128),
        weight_one.reshape(896, 128),
        gain_two.reshape(1, 128),
        weight_two.reshape(896, 128),
        cotangent.reshape(rows, 128),
    )
    out, grad, w1, w2, g1, g2 = pl.pallas_call(
        hand_over,
        out_shape=shapes,
        in_specs=[vmem] * 6,
        out_specs=[hbm] * 6,
        scratch_shapes=[pltpu.SemaphoreType.DMA((6,))],
    )(*[pltpu.with_memory_space_constraint(r, pltpu.VMEM) for r in results])
    return (
        out.reshape(features.shape),
        grad.reshape(features.shape),
        w1.reshape(7, 128, 128),
        w2.reshape(7, 128, 128),
        g1.reshape(128),
        g2.reshape(128),
    )


def solution(mesh):
    bricks = P("shape", "space", None, None)
    in_specs = (
        bricks,
        P(),
        P(),
        P(),
        P(),
        P("shape", "space"),
        bricks,
        P("shape", "space", None),
        bricks,
    )
    out_specs = (bricks, bricks, P(), P(), P(), P())
    return jax.shard_map(shards, mesh=mesh, in_specs=in_specs, out_specs=out_specs, check_vma=False)
```
